32 devices in a mesh: rep: 4 (over z), grp: 8 (over y, x, core).
Axes of the slice: x: 2, y: 2, z: 4, core: 2. Of those that a mesh axis runs over, the one named last changes fastest.
Arguments:
- features: bfloat16 [4096, 256], P(('rep', 'grp')), may hold values from -6 to 6
- weight: bfloat16 [256, 256], replicated, may hold values from -0.375 to 0.375
- bias: float32 [256], replicated, may hold values from -3 to 3
- cotangent: bfloat16 [4096, 256], P(('rep', 'grp')), may hold values from -6 to 6
- degree: int32 [4096], P(('rep', 'grp')), may hold values from 1 to 99
- tile_cols: int32 [32, 24], P(('rep', 'grp')), may hold values from 0 to 23, as said below
- edge_tile: int32 [32, 3840], P(('rep', 'grp')), may hold values from 0 to 23
- edge_row: int32 [32, 3840], P(('rep', 'grp')), may hold values from 0 to 127
- edge_col: int32 [32, 3840], P(('rep', 'grp')), may hold values from 0 to 127
Outputs:
- hidden: bfloat16 [4096, 256], P(('rep', 'grp'))
- grad_features: bfloat16 [4096, 256], P(('rep', 'grp'))
- grad_weight: float32 [256, 256], replicated
- grad_bias: float32 [256], replicated
The draws below stay inside these ranges and needn't reach their ends.
Inputs may be any that keep to these rules, and one draw needn't show every extreme that they name: `tile_cols`: each row lists 8 different tile columns in each of the ranges 0 to 7, 8 to 15 and 16 to 23, in that order.
All inputs are finite; a program needn't handle non-finite values.
Results may differ from the reference program's by a relative error of at most 0.0062.
Values may be sent and summed in bfloat16 or wider, within the bound.
A program may use at most 64 MiB of HBM per device.

```python
import jax
import jax.numpy as jnp
from jax import lax

F = 256
TILE = 128
TPB = 8
TCAP = 24
E_DEV = 3840
NODES = 4096
N_REP = 4
N_GRP = 8
DEVICES = 32


def draw_tile_cols(key, part):
    keys = jax.random.split(jax.random.fold_in(key, 17), DEVICES * 3)
    chosen = jax.vmap(lambda one: jax.random.permutation(one, N_GRP)[:TPB])(keys)
    chosen = chosen.reshape(DEVICES, 3, TPB) + (jnp.arange(3, dtype=jnp.int32) * N_GRP)[None, :, None]
    return chosen.reshape(DEVICES, 3 * TPB).astype(jnp.int32)


def with_ends(drawn, stream_key, low, largest):
    longest = drawn.shape.index(max(drawn.shape))
    spots = []
    for shift in (0, 1):
        where = [jax.random.randint(jax.random.fold_in(stream_key, axis), (), 0, length) for axis, length in enumerate(drawn.shape)]
        where[longest] = (where[longest] + shift) % drawn.shape[longest]
        spots.append(tuple(where))
    return drawn.at[spots[0]].set(low).at[spots[1]].set(largest)


def levels(rng, dims, pieces, low, top_value):
    loudness = 1.0
    for dim, shards_of in pieces:
        draws = jax.random.uniform(jax.random.fold_in(jax.random.fold_in(rng, 6), dim), (shards_of,), jnp.float32, low / len(pieces), top_value / len(pieces))
        loudness = loudness * jnp.repeat(jnp.exp(draws), dims[dim] // shards_of).reshape((-1,) + (1,) * (len(dims) - 1 - dim))
    return loudness


def centred(stream_key, shape, scale, bound, pieces=(), held_as=jnp.bfloat16):
    result = jax.random.normal(stream_key, shape, jnp.float32) * scale
    if len(pieces) > 0:
        result = levels(stream_key, shape, pieces, -0.22, 0.18) * result
    return jnp.clip(result, min=-bound, max=bound).astype(held_as)


def setup_inputs(seed: int = 0) -> dict:
    splits = jax.random.split(jax.random.key(seed), 10)
    return {
        "features": centred(splits[0], (NODES, F), 1.0, 6.0, ((0, 32),)),
        "weight": centred(splits[1], (F, F), F ** -0.5, 0.375),
        "bias": centred(splits[2], (F,), 0.5, 3.0, (), jnp.float32),
        "cotangent": centred(splits[3], (NODES, F), 1.0, 6.0, ((0, 32),)),
        "degree": with_ends(jax.random.randint(splits[4], (NODES,), 1, 100), jax.random.fold_in(splits[4], 1), 1, 99).astype(jnp.int32),
        "tile_cols": draw_tile_cols(jax.random.fold_in(splits[9], 71), 0),
        "edge_tile": with_ends(jax.random.randint(splits[6], (DEVICES, E_DEV), 0, TCAP), jax.random.fold_in(splits[6], 1), 0, TCAP - 1).astype(jnp.int32),
        "edge_row": with_ends(jax.random.randint(splits[7], (DEVICES, E_DEV), 0, TILE), jax.random.fold_in(splits[7], 1), 0, TILE - 1).astype(jnp.int32),
        "edge_col": with_ends(jax.random.randint(splits[8], (DEVICES, E_DEV), 0, TILE), jax.random.fold_in(splits[8], 1), 0, TILE - 1).astype(jnp.int32),
    }


def reference(features, weight, bias, cotangent, degree, tile_cols, edge_tile, edge_row, edge_col):
    block = TILE * N_GRP
    dinv = lax.rsqrt(degree.astype(jnp.float32))
    scaled = (jnp.dot(features, weight, preferred_element_type=jnp.float32) * dinv[:, None]).astype(jnp.bfloat16)
    device_ids = jnp.arange(DEVICES, dtype=jnp.int32)
    columns = jnp.take_along_axis(tile_cols, edge_tile, axis=1)
    source_group = (device_ids[:, None] // N_GRP - 1 + columns // N_GRP) % N_REP
    source = (source_group * block + columns % N_GRP * TILE + edge_col).astype(jnp.int32)
    window = (columns * TILE + edge_col).astype(jnp.int32)

    def forward_one(pair):
        sources, rows = pair
        values = scaled[sources].astype(jnp.float32)
        return jax.ops.segment_sum(values, rows, num_segments=TILE)
    sums = lax.map(forward_one, (source, edge_row)).reshape(NODES, F)
    pre = sums * dinv[:, None] + bias[None, :]
    sig = jax.nn.sigmoid(pre)
    hidden = (pre * sig).astype(jnp.bfloat16)
    grad_pre = cotangent.astype(jnp.float32) * sig * (1.0 + pre * (1.0 - sig))
    back = (grad_pre * dinv[:, None]).astype(jnp.bfloat16).reshape(DEVICES, TILE, F)

    def backward_one(total, index):
        rows = edge_row[index]
        values = back[index][rows].astype(jnp.float32)
        part = jax.ops.segment_sum(values, window[index], num_segments=3 * block)
        first = lax.optimization_barrier(part[:block].astype(jnp.bfloat16)).astype(jnp.float32)
        last = lax.optimization_barrier(part[2 * block:].astype(jnp.bfloat16)).astype(jnp.float32)
        group = index // N_GRP
        total = total.at[(group - 1) % N_REP].add(first)
        total = total.at[group].add(part[block:2 * block])
        total = total.at[(group + 1) % N_REP].add(last)
        return (total, None)
    start = jnp.zeros((N_REP, block, F), jnp.float32)
    grad_sum, unused = lax.scan(backward_one, start, device_ids)
    grad_scaled = (grad_sum.reshape(NODES, F) * dinv[:, None]).astype(jnp.bfloat16)
    grad_features = jnp.dot(grad_scaled, weight.T, preferred_element_type=jnp.float32).astype(jnp.bfloat16)
    grad_weight = jnp.dot(features.T, grad_scaled, preferred_element_type=jnp.float32)
    grad_bias = lax.optimization_barrier(jnp.sum(grad_pre, axis=0))
    return (hidden, grad_features, grad_weight, grad_bias)
```

```python
import functools

import jax
import jax.numpy as jnp
from jax import lax
from jax.experimental import pallas as pl
from jax.experimental.pallas import tpu as pltpu
from jax.sharding import PartitionSpec as P

MESH = pl.DeviceIdType.MESH
F32 = jnp.float32
BF16 = jnp.bfloat16
ROWS = (((0,), (0,)), ((), ()))
LANES = (((1,), (1,)), ((), ()))


def mm(a, b, dims=(((1,), (0,)), ((), ()))):
    return lax.dot_general(a, b, dims, preferred_element_type=F32)


def kernel(
    reps,
    members,
    cols_ref,
    features_ref,
    weight_ref,
    bias_ref,
    cotangent_ref,
    degree_ref,
    edge_tile_ref,
    edge_row_ref,
    edge_col_ref,
    hidden_ref,
    grad_features_ref,
    grad_weight_ref,
    grad_bias_ref,
    left_hot,
    right_hot,
    tiles_out,
    tiles,
    tiles_t,
    scaled,
    sums_out,
    sums,
    back,
    parts_out,
    parts,
    local_weight,
    weight_out,
    weight_in,
    piece_out,
    piece_in,
    whole,
    grp_send,
    grp_recv,
    rep_send,
    rep_recv,
    near_send,
    near_recv,
):
    rep = lax.axis_index("rep")
    me = lax.axis_index("grp")
    tile = features_ref.shape[0]
    width = weight_ref.shape[1]
    piece = weight_ref.shape[0] // members

    def mate(o):
        return lax.rem(me + o, members)

    def peer(o):
        return lax.rem(rep + o, reps)

    barrier = pltpu.get_barrier_semaphore()
    for o in range(1, members):
        pl.semaphore_signal(barrier, inc=1, device_id={"grp": mate(o)}, device_id_type=MESH)
    for o in range(1, reps):
        pl.semaphore_signal(barrier, inc=1, device_id={"rep": peer(o)}, device_id_type=MESH)

    sends = []

    def to_mate(stage, o, src, dst):
        copy = pltpu.make_async_remote_copy(
            src_ref=src,
            dst_ref=dst,
            send_sem=grp_send.at[stage, o],
            recv_sem=grp_recv.at[stage, o],
            device_id={"grp": mate(o)},
            device_id_type=MESH,
        )
        copy.start()
        sends.append(copy)
        return copy

    def to_near(slot, o, src, dst):
        copy = pltpu.make_async_remote_copy(
            src_ref=src,
            dst_ref=dst,
            send_sem=near_send.at[slot],
            recv_sem=near_recv.at[slot],
            device_id={"rep": peer(o)},
            device_id_type=MESH,
        )
        copy.start()
        sends.append(copy)
        return copy

    dinv = lax.rsqrt(degree_ref[...].astype(F32))
    dinv = jnp.broadcast_to(dinv, (tile, tile)).T
    dinv = jnp.concatenate([dinv] * (width // tile), axis=1)

    own = pl.ds(tile, tile)
    scaled[own, :] = (mm(features_ref[...], weight_ref[...]) * dinv).astype(BF16)
    pl.semaphore_wait(barrier, members + reps - 2)
    near = [
        to_near(0, 1, scaled.at[own], scaled.at[pl.ds(0, tile)]),
        to_near(1, reps - 1, scaled.at[own], scaled.at[pl.ds(2 * tile, tile)]),
    ]

    listed = edge_tile_ref[...]
    column = jnp.zeros_like(listed)
    for t in range(cols_ref.shape[1]):
        column = jnp.where(listed == t, cols_ref[0, t], column)
    part = (column >= members).astype(jnp.int32) + (column >= 2 * members).astype(jnp.int32)
    offset = column - part * members - me
    offset = jnp.where(offset < 0, offset + members, offset)
    left_key = offset * tile + edge_row_ref[...]
    right_key = part * tile + edge_col_ref[...]
    edges = listed.shape[1]
    step = 32

    def one_hot(ref, key, rows, first):
        def body(i, _):
            at = pl.multiple_of(i * step, step)
            spot = lax.broadcasted_iota(jnp.int32, (step, edges), 0) + (at + first)
            ref[pl.ds(at, step), :] = jnp.where(spot == key, 1.0, 0.0).astype(BF16)
            return 0

        lax.fori_loop(0, rows // step, body, 0)

    one_hot(right_hot, right_key, 3 * tile, 0)
    batch = left_hot.shape[0] // tile
    tile_copies = {}
    for first in range(0, members, batch):
        one_hot(left_hot, left_key, batch * tile, first * tile)
        counts = mm(left_hot[...], right_hot[...], LANES).astype(BF16)
        for o in range(first, first + batch):
            block = counts[(o - first) * tile : (o - first + 1) * tile]
            if o == 0:
                tiles[0] = block
            else:
                tiles_out[o] = block
                tile_copies[o] = to_mate(0, o, tiles_out.at[o], tiles.at[o])

    for copy in near:
        copy.wait_recv()
    sum_copies = []
    for o in range(1, members):
        tile_copies[o].wait_recv()
        sums_out[o] = mm(tiles[o], scaled[...]).astype(BF16)
        back_to = members - o
        sum_copies.append((back_to, to_mate(1, back_to, sums_out.at[o], sums.at[back_to])))
    total = mm(tiles[0], scaled[...])
    for o in range(members):
        tiles_t[:, pl.ds(o * tile, tile)] = tiles[o].T
    for o, copy in sum_copies:
        copy.wait_recv()
        total = total + sums[o].astype(F32)
    pre = total * dinv + bias_ref[...]
    sig = jax.nn.sigmoid(pre)
    grad_pre = cotangent_ref[...].astype(F32) * sig * (1.0 + pre * (1.0 - sig))
    back[pl.ds(0, tile), :] = (grad_pre * dinv).astype(BF16)
    back_copies = [
        to_mate(2, o, back.at[pl.ds(0, tile)], back.at[pl.ds(o * tile, tile)])
        for o in range(1, members)
    ]
    hidden_ref[...] = (pre * sig).astype(BF16)
    bias_part = jnp.sum(grad_pre, axis=0, keepdims=True)

    for copy in back_copies:
        copy.wait_recv()
    grads = mm(tiles_t[...], back[...])
    parts_out[pl.ds(0, tile), :] = grads[:tile].astype(BF16)
    parts_out[pl.ds(tile, tile), :] = grads[2 * tile :].astype(BF16)
    lower, upper = pl.ds(0, tile), pl.ds(tile, tile)
    near = [
        to_near(2, reps - 1, parts_out.at[lower], parts.at[lower]),
        to_near(3, 1, parts_out.at[upper], parts.at[upper]),
    ]
    for copy in near:
        copy.wait_recv()
    grad_sum = grads[tile : 2 * tile] + parts[lower, :].astype(F32) + parts[upper, :].astype(F32)
    grad_scaled = (grad_sum * dinv).astype(BF16)

    local_weight[...] = mm(features_ref[...], grad_scaled, ROWS)
    bias_rows = jnp.broadcast_to(bias_part, (8, width))
    copies = []
    for o in range(members):
        start = pl.multiple_of(mate(o) * piece, piece)
        weight_out[o, pl.ds(0, piece), :] = local_weight[pl.ds(start, piece), :]
        weight_out[o, pl.ds(piece, 8), :] = bias_rows
        if o:
            copies.append(to_mate(3, o, weight_out.at[o], weight_in.at[o]))
    grad_features_ref[...] = mm(grad_scaled, weight_ref[...], LANES).astype(BF16)
    total = weight_out[0]
    for o, copy in enumerate(copies, 1):
        copy.wait_recv()
        total = total + weight_in[o]
    piece_out[...] = total
    copies = []
    for o in range(1, reps):
        copy = pltpu.make_async_remote_copy(
            src_ref=piece_out,
            dst_ref=piece_in.at[o],
            send_sem=rep_send.at[o],
            recv_sem=rep_recv.at[o],
            device_id={"rep": peer(o)},
            device_id_type=MESH,
        )
        copy.start()
        sends.append(copy)
        copies.append(copy)
    for o, copy in enumerate(copies, 1):
        copy.wait_recv()
        total = total + piece_in[o]
    here = pl.ds(pl.multiple_of(me * piece, piece), piece)
    whole[here, :] = total[:piece]
    grad_bias_ref[...] = total[piece : piece + 1]
    copies = [to_mate(4, o, whole.at[here], whole.at[here]) for o in range(1, members)]
    for copy in copies:
        copy.wait_recv()
    grad_weight_ref[...] = whole[...]
    for copy in sends:
        copy.wait_send()


def per_device(
    reps, members, features, weight, bias, cotangent, degree, cols, edge_tile, edge_row, edge_col
):
    tile, width = features.shape
    depth = weight.shape[0]
    edges = edge_tile.shape[1]
    piece = depth // members
    batch = 4 if members % 4 == 0 else 1
    vmem = pl.BlockSpec(memory_space=pltpu.VMEM)
    smem = pl.BlockSpec(memory_space=pltpu.SMEM)
    hidden, grad_features, grad_weight, grad_bias = pl.pallas_call(
        functools.partial(kernel, reps, members),
        out_shape=(
            jax.ShapeDtypeStruct((tile, width), BF16),
            jax.ShapeDtypeStruct((tile, depth), BF16),
            jax.ShapeDtypeStruct((depth, width), F32),
            jax.ShapeDtypeStruct((1, width), F32),
        ),
        in_specs=[smem] + [vmem] * 8,
        out_specs=(vmem,) * 4,
        scratch_shapes=[
            pltpu.VMEM((batch * tile, edges), BF16),
            pltpu.VMEM((3 * tile, edges), BF16),
            pltpu.VMEM((members, tile, 3 * tile), BF16),
            pltpu.VMEM((members, tile, 3 * tile), BF16),
            pltpu.VMEM((3 * tile, members * tile), BF16),
            pltpu.VMEM((3 * tile, width), BF16),
            pltpu.VMEM((members, tile, width), BF16),
            pltpu.VMEM((members, tile, width), BF16),
            pltpu.VMEM((members * tile, width), BF16),
            pltpu.VMEM((2 * tile, width), BF16),
            pltpu.VMEM((2 * tile, width), BF16),
            pltpu.VMEM((depth, width), F32),
            pltpu.VMEM((members, piece + 8, width), F32),
            pltpu.VMEM((members, piece + 8, width), F32),
            pltpu.VMEM((piece + 8, width), F32),
            pltpu.VMEM((reps, piece + 8, width), F32),
            pltpu.VMEM((depth, width), F32),
            pltpu.SemaphoreType.DMA((5, members)),
            pltpu.SemaphoreType.DMA((5, members)),
            pltpu.SemaphoreType.DMA((reps,)),
            pltpu.SemaphoreType.DMA((reps,)),
            pltpu.SemaphoreType.DMA((4,)),
            pltpu.SemaphoreType.DMA((4,)),
        ],
        compiler_params=pltpu.CompilerParams(
            collective_id=0, has_side_effects=True, vmem_limit_bytes=48 * 2**20
        ),
    )(
        cols,
        features,
        weight,
        bias[None, :],
        cotangent,
        degree[None, :],
        edge_tile,
        edge_row,
        edge_col,
    )
    return hidden, grad_features, grad_weight, grad_bias[0]


def solution(mesh):
    nodes = P(("rep", "grp"), None)
    return jax.shard_map(
        functools.partial(per_device, mesh.shape["rep"], mesh.shape["grp"]),
        mesh=mesh,
        in_specs=(nodes, P(), P(), nodes, P(("rep", "grp")), nodes, nodes, nodes, nodes),
        out_specs=(nodes, nodes, P(), P()),
        check_vma=False,
    )
```

```python
import functools

import jax
import jax.numpy as jnp
from jax import lax
from jax.experimental import pallas as pl
from jax.experimental.pallas import tpu as pltpu
from jax.sharding import PartitionSpec as P

MESH = pl.DeviceIdType.MESH
F32 = jnp.float32
BF16 = jnp.bfloat16
ROWS = (((0,), (0,)), ((), ()))
LANES = (((1,), (1,)), ((), ()))


def mm(a, b, dims=(((1,), (0,)), ((), ()))):
    return lax.dot_general(a, b, dims, preferred_element_type=F32)


def kernel(
    reps,
    members,
    cols_hbm,
    features_hbm,
    weight_hbm,
    bias_hbm,
    cotangent_hbm,
    degree_hbm,
    edge_tile_hbm,
    edge_row_hbm,
    edge_col_hbm,
    hidden_ref,
    grad_features_ref,
    grad_weight_ref,
    grad_bias_ref,
    cols_ref,
    features_ref,
    weight_ref,
    bias_ref,
    cotangent_ref,
    degree_ref,
    edge_tile_ref,
    edge_row_ref,
    edge_col_ref,
    load_sem,
    spots,
    left_hot,
    right_hot,
    listed,
    tiles_t,
    scaled,
    sums_out,
    sums,
    back,
    parts_out,
    parts,
    local_weight,
    weight_out,
    weight_in,
    piece_out,
    piece_in,
    whole,
    grp_send,
    grp_recv,
    rep_send,
    rep_recv,
    near_send,
    near_recv,
):
    rep = lax.axis_index("rep")
    me = lax.axis_index("grp")
    tile, width = features_ref.shape
    half = tile // 2
    edges = edge_tile_ref.shape[1]
    piece = whole.shape[1]
    chips = members // 2
    chip, core = me // 2, me % 2

    def mate(o):
        d, s = o // 2, o % 2
        return (chip + d) % chips * 2 + (core + s) % 2

    def source(o):
        d, s = o // 2, o % 2
        return (chip + chips - d) % chips * 2 + (core + s) % 2

    def reply(o):
        return (chips - o // 2) % chips * 2 + o % 2

    def peer(o):
        return (rep + o) % reps

    barrier = pltpu.get_barrier_semaphore()
    for o in range(1, members):
        pl.semaphore_signal(barrier, inc=1, device_id={"grp": mate(o)}, device_id_type=MESH)
    for o in range(1, reps):
        pl.semaphore_signal(barrier, inc=1, device_id={"rep": peer(o)}, device_id_type=MESH)
    pairs = (
        (cols_hbm, cols_ref),
        (edge_tile_hbm, edge_tile_ref),
        (edge_row_hbm, edge_row_ref),
        (edge_col_hbm, edge_col_ref),
        (features_hbm, features_ref),
        (weight_hbm, weight_ref),
        (degree_hbm, degree_ref),
        (bias_hbm, bias_ref),
        (cotangent_hbm, cotangent_ref),
    )
    loads = [
        pltpu.make_async_copy(a, b, load_sem.at[i]) for i, (a, b) in enumerate(pairs)
    ]
    for load in loads:
        load.start()

    def remote(src, dst, send, recv, to):
        return pltpu.make_async_remote_copy(
            src_ref=src,
            dst_ref=dst,
            send_sem=send,
            recv_sem=recv,
            device_id=to,
            device_id_type=MESH,
        )

    def to_mate(stage, o, src, dst):
        send, recv = grp_send.at[stage, o], grp_recv.at[stage, o]
        return remote(src, dst, send, recv, {"grp": mate(o)})

    def to_near(slot, o, src, dst):
        return remote(src, dst, near_send.at[slot], near_recv.at[slot], {"rep": peer(o)})

    def begin(copies):
        for copy in copies:
            copy.start()
        return copies

    for load in loads[:4]:
        load.wait()
    edge_tile = edge_tile_ref[...]
    column = jnp.zeros_like(edge_tile)
    for t in range(cols_ref.shape[1]):
        column = jnp.where(edge_tile == t, cols_ref[0, t], column)
    listed[0, pl.ds(0, 1), :] = edge_row_ref[...]
    listed[0, pl.ds(1, 1), :] = column * tile + edge_col_ref[...]
    pl.semaphore_wait(barrier, members + reps - 2)
    edge_copies = begin(
        [to_mate(0, o, listed.at[0], listed.at[o]) for o in range(1, members)]
    )

    for load in loads[4:]:
        load.wait()
    dinv = lax.rsqrt(degree_ref[...].astype(F32))
    dinv = jnp.broadcast_to(dinv, (tile, tile)).T
    dinv = jnp.concatenate([dinv] * (width // tile), axis=1)

    own = pl.ds(tile, tile)
    scaled[own, :] = (mm(features_ref[...], weight_ref[...]) * dinv).astype(BF16)
    scaled_copies = begin(
        [
            to_near(0, 1, scaled.at[own], scaled.at[pl.ds(0, tile)]),
            to_near(1, reps - 1, scaled.at[own], scaled.at[pl.ds(2 * tile, tile)]),
        ]
    )
    spots[...] = lax.broadcasted_iota(jnp.int32, spots.shape, 0).astype(F32).astype(BF16)

    span = edges // 5 if edges % 640 == 0 else edges

    def count(o):
        row = listed[o, pl.ds(0, 1), :]
        window = listed[o, pl.ds(1, 1), :]
        column = window // tile
        part = (column >= members).astype(jnp.int32) + (column >= 2 * members).astype(jnp.int32)
        place = window - column * tile
        upper = (place >= half).astype(jnp.int32)
        left = jnp.where(column - part * members == me, upper * tile + row, -1)
        right = part * half + place - upper * half
        total = None
        for first in range(0, edges, span):
            at = pl.ds(first, span)
            for hot, key in ((left_hot, left), (right_hot, right)):
                rows = hot.shape[0]
                key = key[:, first : first + span].astype(F32)
                key = jnp.broadcast_to(key, (16, span)).astype(BF16)
                key = jnp.concatenate([key] * (rows // 16), axis=0)
                spot = jnp.concatenate([spots[:rows]] * (span // 128), axis=1)
                hot[:, at] = jnp.where(spot == key, jnp.ones_like(key), jnp.zeros_like(key))
            term = mm(right_hot[:, at], left_hot[:, at], LANES)
            total = term if total is None else total + term
        total = total.astype(BF16)
        blocks = [
            total[p * half : (p + 1) * half, u * tile : (u + 1) * tile]
            for p in range(3)
            for u in range(2)
        ]
        return jnp.concatenate(blocks, axis=0)

    counts = count(0)
    tiles_t[0] = counts
    for copy in scaled_copies:
        copy.wait_recv()
    total = mm(counts, scaled[...], ROWS)

    def sum_copy(o):
        return to_mate(1, reply(o), sums_out.at[o], sums.at[reply(o)])

    def forward(o, _):
        to_mate(0, o, listed.at[0], listed.at[o]).wait_recv()
        counts = count(o)
        tiles_t[o] = counts
        sums_out[o] = mm(counts, scaled[...], ROWS).astype(BF16)
        sum_copy(o).start()
        return 0

    lax.fori_loop(1, members, forward, 0)
    for o in range(1, members):
        to_mate(1, o, sums_out.at[o], sums.at[o]).wait_recv()
        total = total + sums[o].astype(F32)
    pre = total * dinv + bias_ref[...]
    sig = jax.nn.sigmoid(pre)
    grad_pre = cotangent_ref[...].astype(F32) * sig * (1.0 + pre * (1.0 - sig))
    back[0] = (grad_pre * dinv).astype(BF16)
    across = [to_mate(2, o, back.at[0], back.at[o]) for o in range(2, members, 2)]
    beside = [to_mate(2, 1, back.at[0], back.at[1])]
    begin(across)
    begin(beside)
    hidden_ref[...] = (pre * sig).astype(BF16)
    bias_part = jnp.sum(grad_pre, axis=0, keepdims=True)

    grads = mm(tiles_t[0], back[0])
    for d in range(1, chips):
        across[d - 1].wait_recv()
        copy = remote(
            back.at[2 * d],
            back.at[2 * d + 1],
            grp_send.at[2, 2 * d + 1],
            grp_recv.at[2, 2 * d + 1],
            {"grp": mate(1)},
        )
        copy.start()
        beside.append(copy)
        grads = grads + mm(tiles_t[2 * d], back[2 * d])
    for d in range(chips):
        beside[d].wait_recv()
        grads = grads + mm(tiles_t[2 * d + 1], back[2 * d + 1])
    parts_out[pl.ds(0, tile), :] = grads[:tile].astype(BF16)
    parts_out[pl.ds(tile, tile), :] = grads[2 * tile :].astype(BF16)
    lower, upper = pl.ds(0, tile), pl.ds(tile, tile)
    part_copies = begin(
        [
            to_near(2, reps - 1, parts_out.at[lower], parts.at[lower]),
            to_near(3, 1, parts_out.at[upper], parts.at[upper]),
        ]
    )
    for copy in part_copies:
        copy.wait_recv()
    grad_sum = grads[tile : 2 * tile] + parts[lower, :].astype(F32) + parts[upper, :].astype(F32)
    grad_scaled = (grad_sum * dinv).astype(BF16)

    local_weight[...] = mm(features_ref[...], grad_scaled, ROWS)
    bias_rows = jnp.broadcast_to(bias_part, (8, width))
    extra = weight_out.shape[1] - piece
    weight_copies = []
    for o in range(members):
        start = pl.multiple_of(mate(o) * piece, piece)
        block = jnp.concatenate(
            [local_weight[pl.ds(start, piece), :]] + [bias_rows] * (extra // 8), axis=0
        )
        if o == 0:
            total = block
        else:
            weight_out[o] = block.astype(BF16)
            weight_copies += begin([to_mate(3, o, weight_out.at[o], weight_in.at[o])])
    grad_features_ref[...] = mm(grad_scaled, weight_ref[...], LANES).astype(BF16)
    for o, copy in enumerate(weight_copies, 1):
        copy.wait_recv()
        total = total + weight_in[o].astype(F32)
    piece_out[...] = total
    piece_copies = begin(
        [
            remote(piece_out, piece_in.at[o], rep_send.at[o], rep_recv.at[o], {"rep": peer(o)})
            for o in range(1, reps)
        ]
    )
    for o, copy in enumerate(piece_copies, 1):
        copy.wait_recv()
        total = total + piece_in[o]
    whole[me] = total[:piece].astype(whole.dtype)
    grad_bias_ref[...] = total[piece : piece + 1]
    whole_copies = begin(
        [to_mate(4, o, whole.at[me], whole.at[me]) for o in range(1, members)]
    )
    for copy in whole_copies:
        copy.wait_recv()
    grad_weight_ref[...] = whole[...].astype(F32).reshape(grad_weight_ref.shape)

    for copies in (
        edge_copies,
        scaled_copies,
        across,
        beside,
        part_copies,
        weight_copies,
        piece_copies,
        whole_copies,
    ):
        for copy in copies:
            copy.wait_send()
    for o in range(1, members):
        sum_copy(o).wait_send()


def per_device(
    reps, members, features, weight, bias, cotangent, degree, cols, edge_tile, edge_row, edge_col
):
    tile, width = features.shape
    depth = weight.shape[0]
    edges = edge_tile.shape[1]
    piece = depth // members
    tail = piece + 16 - piece % 16
    args = (cols, features, weight, bias[None, :], cotangent, degree[None, :])
    args += (edge_tile, edge_row, edge_col)
    vmem = pl.BlockSpec(memory_space=pltpu.VMEM)
    hbm = pl.BlockSpec(memory_space=pltpu.HBM)
    hidden, grad_features, grad_weight, grad_bias = pl.pallas_call(
        functools.partial(kernel, reps, members),
        out_shape=(
            jax.ShapeDtypeStruct((tile, width), BF16),
            jax.ShapeDtypeStruct((tile, depth), BF16),
            jax.ShapeDtypeStruct((depth, width), F32),
            jax.ShapeDtypeStruct((1, width), F32),
        ),
        in_specs=[hbm] * len(args),
        out_specs=(vmem,) * 4,
        scratch_shapes=[pltpu.SMEM(cols.shape, cols.dtype)]
        + [pltpu.VMEM(a.shape, a.dtype) for a in args[1:]]
        + [
            pltpu.SemaphoreType.DMA((len(args),)),
            pltpu.VMEM((2 * tile, 128), BF16),
            pltpu.VMEM((2 * tile, edges), BF16),
            pltpu.VMEM((3 * tile // 2, edges), BF16),
            pltpu.VMEM((members, 2, edges), jnp.int32),
            pltpu.VMEM((members, 3 * tile, tile), BF16),
            pltpu.VMEM((3 * tile, width), BF16),
            pltpu.VMEM((members, tile, width), BF16),
            pltpu.VMEM((members, tile, width), BF16),
            pltpu.VMEM((members, tile, width), BF16),
            pltpu.VMEM((2 * tile, width), BF16),
            pltpu.VMEM((2 * tile, width), BF16),
            pltpu.VMEM((depth, width), F32),
            pltpu.VMEM((members, tail, width), BF16),
            pltpu.VMEM((members, tail, width), BF16),
            pltpu.VMEM((tail, width), F32),
            pltpu.VMEM((reps, tail, width), F32),
            pltpu.VMEM((members, piece, width), BF16),
            pltpu.SemaphoreType.DMA((5, members)),
            pltpu.SemaphoreType.DMA((5, members)),
            pltpu.SemaphoreType.DMA((reps,)),
            pltpu.SemaphoreType.DMA((reps,)),
            pltpu.SemaphoreType.DMA((4,)),
            pltpu.SemaphoreType.DMA((4,)),
        ],
        compiler_params=pltpu.CompilerParams(
            collective_id=0, has_side_effects=True, vmem_limit_bytes=48 * 2**20
        ),
    )(*args)
    return hidden, grad_features, grad_weight, grad_bias[0]


def solution(mesh):
    nodes = P(("rep", "grp"), None)
    return jax.shard_map(
        functools.partial(per_device, mesh.shape["rep"], mesh.shape["grp"]),
        mesh=mesh,
        in_specs=(nodes, P(), P(), nodes, P(("rep", "grp")), nodes, nodes, nodes, nodes),
        out_specs=(nodes, nodes, P(), P()),
        check_vma=False,
    )
```

```python
import functools

import jax
import jax.numpy as jnp
from jax import lax
from jax.experimental import pallas as pl
from jax.experimental.pallas import tpu as pltpu
from jax.sharding import PartitionSpec as P

MESH = pl.DeviceIdType.MESH
F32 = jnp.float32
BF16 = jnp.bfloat16
LIMIT = 63 * 2**20
ROWS = (((0,), (0,)), ((), ()))
LANES = (((1,), (1,)), ((), ()))


def mm(a, b, dims=(((1,), (0,)), ((), ()))):
    return lax.dot_general(a, b, dims, preferred_element_type=F32)


def kernel(
    reps,
    members,
    cols_hbm,
    features_hbm,
    weight_hbm,
    bias_hbm,
    cotangent_hbm,
    degree_hbm,
    edge_tile_hbm,
    edge_row_hbm,
    edge_col_hbm,
    hidden_hbm,
    grad_features_hbm,
    grad_weight_hbm,
    grad_bias_hbm,
    cols_ref,
    features_ref,
    weight_ref,
    bias_ref,
    cotangent_ref,
    degree_ref,
    edge_tile_ref,
    edge_row_ref,
    edge_col_ref,
    hidden_ref,
    grad_features_ref,
    grad_weight_ref,
    grad_bias_ref,
    load_sem,
    store_sem,
    spots,
    left_hot,
    right_hot,
    listed,
    tiles_t,
    scaled,
    sums_out,
    sums,
    back,
    parts_out,
    parts,
    local_weight,
    weight_out,
    weight_in,
    piece_out,
    piece_in,
    whole,
    bias_out,
    bias_in,
    bias_sum,
    bias_near,
    grp_send,
    grp_recv,
    rep_send,
    rep_recv,
    near_send,
    near_recv,
):
    rep = lax.axis_index("rep")
    me = lax.axis_index("grp")
    tile, width = features_ref.shape
    half = tile // 2
    edges = edge_tile_ref.shape[1]
    piece = whole.shape[1]
    chips = members // 2
    chip, core = me // 2, me % 2

    def mate(o):
        d, s = o // 2, o % 2
        return (chip + d) % chips * 2 + (core + s) % 2

    def source(o):
        d, s = o // 2, o % 2
        return (chip + chips - d) % chips * 2 + (core + s) % 2

    def reply(o):
        return (chips - o // 2) % chips * 2 + o % 2

    def peer(o):
        return (rep + o) % reps

    barrier = pltpu.get_barrier_semaphore()
    for o in range(1, members):
        pl.semaphore_signal(barrier, inc=1, device_id={"grp": mate(o)}, device_id_type=MESH)
    for o in range(1, reps):
        pl.semaphore_signal(barrier, inc=1, device_id={"rep": peer(o)}, device_id_type=MESH)
    pairs = (
        (cols_hbm, cols_ref),
        (edge_tile_hbm, edge_tile_ref),
        (edge_row_hbm, edge_row_ref),
        (edge_col_hbm, edge_col_ref),
        (features_hbm, features_ref),
        (weight_hbm, weight_ref),
        (degree_hbm, degree_ref),
        (bias_hbm, bias_ref),
        (cotangent_hbm, cotangent_ref),
    )
    loads = [
        pltpu.make_async_copy(a, b, load_sem.at[i]) for i, (a, b) in enumerate(pairs)
    ]
    for load in loads:
        load.start()

    def remote(src, dst, send, recv, to):
        return pltpu.make_async_remote_copy(
            src_ref=src,
            dst_ref=dst,
            send_sem=send,
            recv_sem=recv,
            device_id=to,
            device_id_type=MESH,
        )

    def to_mate(stage, o, src, dst):
        send, recv = grp_send.at[stage, o], grp_recv.at[stage, o]
        return remote(src, dst, send, recv, {"grp": mate(o)})

    def to_near(slot, o, src, dst):
        return remote(src, dst, near_send.at[slot], near_recv.at[slot], {"rep": peer(o)})

    def store(i, src, dst):
        copy = pltpu.make_async_copy(src, dst, store_sem.at[i])
        copy.start()
        return copy

    def begin(copies):
        for copy in copies:
            copy.start()
        return copies

    for load in loads[:4]:
        load.wait()
    edge_tile = edge_tile_ref[...]
    column = jnp.zeros_like(edge_tile)
    for t in range(cols_ref.shape[1]):
        column = jnp.where(edge_tile == t, cols_ref[0, t], column)
    listed[0, pl.ds(0, 1), :] = edge_row_ref[...]
    listed[0, pl.ds(1, 1), :] = column * tile + edge_col_ref[...]
    pl.semaphore_wait(barrier, members + reps - 2)
    edge_copies = begin(
        [to_mate(0, o, listed.at[0], listed.at[o]) for o in range(1, members)]
    )

    for load in loads[4:]:
        load.wait()
    dinv = lax.rsqrt(degree_ref[...].astype(F32))
    dinv = jnp.broadcast_to(dinv, (tile, tile)).T
    dinv = jnp.concatenate([dinv] * (width // tile), axis=1)

    own = pl.ds(tile, tile)
    scaled[own, :] = (mm(features_ref[...], weight_ref[...]) * dinv).astype(BF16)
    scaled_copies = begin(
        [
            to_near(0, 1, scaled.at[own], scaled.at[pl.ds(0, tile)]),
            to_near(1, reps - 1, scaled.at[own], scaled.at[pl.ds(2 * tile, tile)]),
        ]
    )
    spots[...] = lax.broadcasted_iota(jnp.int32, spots.shape, 0).astype(F32).astype(BF16)

    span = edges // 5 if edges % 640 == 0 else edges

    def count(o):
        row = listed[o, pl.ds(0, 1), :]
        window = listed[o, pl.ds(1, 1), :]
        column = window // tile
        part = (column >= members).astype(jnp.int32) + (column >= 2 * members).astype(jnp.int32)
        place = window - column * tile
        upper = (place >= half).astype(jnp.int32)
        left = jnp.where(column - part * members == me, upper * tile + row, -1)
        right = part * half + place - upper * half
        total = None
        for first in range(0, edges, span):
            at = pl.ds(first, span)
            for hot, key in ((left_hot, left), (right_hot, right)):
                rows = hot.shape[0]
                key = key[:, first : first + span].astype(F32)
                key = jnp.broadcast_to(key, (16, span)).astype(BF16)
                key = jnp.concatenate([key] * (rows // 16), axis=0)
                spot = jnp.concatenate([spots[:rows]] * (span // 128), axis=1)
                hot[:, at] = jnp.where(spot == key, jnp.ones_like(key), jnp.zeros_like(key))
            term = mm(right_hot[:, at], left_hot[:, at], LANES)
            total = term if total is None else total + term
        total = total.astype(BF16)
        blocks = [
            total[p * half : (p + 1) * half, u * tile : (u + 1) * tile]
            for p in range(3)
            for u in range(2)
        ]
        return jnp.concatenate(blocks, axis=0)

    counts = count(0)
    tiles_t[0] = counts
    for copy in scaled_copies:
        copy.wait_recv()
    total = mm(counts, scaled[...], ROWS)

    def sum_copy(o):
        return to_mate(1, reply(o), sums_out.at[o], sums.at[reply(o)])

    def forward(o, _):
        to_mate(0, o, listed.at[0], listed.at[o]).wait_recv()
        counts = count(o)
        tiles_t[o] = counts
        sums_out[o] = mm(counts, scaled[...], ROWS).astype(BF16)
        sum_copy(o).start()
        return 0

    lax.fori_loop(1, members, forward, 0)
    for o in range(1, members):
        to_mate(1, o, sums_out.at[o], sums.at[o]).wait_recv()
        total = total + sums[o].astype(F32)
    pre = total * dinv + bias_ref[...]
    sig = jax.nn.sigmoid(pre)
    grad_pre = cotangent_ref[...].astype(F32) * sig * (1.0 + pre * (1.0 - sig))
    back[0] = (grad_pre * dinv).astype(BF16)
    across = [to_mate(2, o, back.at[0], back.at[o]) for o in range(2, members, 2)]
    beside = [to_mate(2, 1, back.at[0], back.at[1])]
    begin(across)
    begin(beside)
    hidden_ref[...] = (pre * sig).astype(BF16)
    stores = [store(0, hidden_ref, hidden_hbm)]
    bias_out[...] = jnp.broadcast_to(jnp.sum(grad_pre, axis=0, keepdims=True), bias_out.shape)
    bias_copies = begin([to_mate(3, o, bias_out, bias_in.at[o]) for o in range(1, members)])

    grads = mm(tiles_t[0], back[0])
    for d in range(1, chips):
        across[d - 1].wait_recv()
        copy = remote(
            back.at[2 * d],
            back.at[2 * d + 1],
            grp_send.at[2, 2 * d + 1],
            grp_recv.at[2, 2 * d + 1],
            {"grp": mate(1)},
        )
        copy.start()
        beside.append(copy)
        grads = grads + mm(tiles_t[2 * d], back[2 * d])
    for d in range(chips):
        beside[d].wait_recv()
        grads = grads + mm(tiles_t[2 * d + 1], back[2 * d + 1])
    parts_out[pl.ds(0, tile), :] = grads[:tile].astype(BF16)
    parts_out[pl.ds(tile, tile), :] = grads[2 * tile :].astype(BF16)
    lower, upper = pl.ds(0, tile), pl.ds(tile, tile)
    part_copies = begin(
        [
            to_near(2, reps - 1, parts_out.at[lower], parts.at[lower]),
            to_near(3, 1, parts_out.at[upper], parts.at[upper]),
        ]
    )
    bias_total = bias_out[...]
    for o, copy in enumerate(bias_copies, 1):
        copy.wait_recv()
        bias_total = bias_total + bias_in[o]
    bias_sum[...] = bias_total
    bias_copies += begin(
        [
            remote(bias_sum, bias_near.at[o], rep_send.at[1, o], rep_recv.at[1, o], {"rep": peer(o)})
            for o in range(1, reps)
        ]
    )
    for copy in part_copies:
        copy.wait_recv()
    grad_sum = grads[tile : 2 * tile] + parts[lower, :].astype(F32) + parts[upper, :].astype(F32)
    grad_scaled = (grad_sum * dinv).astype(BF16)

    local_weight[...] = mm(features_ref[...], grad_scaled, ROWS)
    weight_copies = []
    for o in list(range(1, members)) + [0]:
        start = pl.multiple_of(mate(o) * piece, piece)
        block = local_weight[pl.ds(start, piece), :]
        if o == 0:
            total = block
        else:
            weight_out[o] = block.astype(BF16)
            weight_copies += begin([to_mate(4, o, weight_out.at[o], weight_in.at[o])])
    grad_features_ref[...] = mm(grad_scaled, weight_ref[...], LANES).astype(BF16)
    stores.append(store(1, grad_features_ref, grad_features_hbm))
    for o, copy in enumerate(bias_copies[members - 1 :], 1):
        copy.wait_recv()
        bias_total = bias_total + bias_near[o]
    grad_bias_ref[...] = bias_total[:1]
    stores.append(store(2, grad_bias_ref, grad_bias_hbm))
    for o, copy in enumerate(weight_copies, 1):
        copy.wait_recv()
        total = total + weight_in[o].astype(F32)
    piece_out[...] = total.astype(BF16)
    piece_copies = begin(
        [
            remote(
                piece_out, piece_in.at[o], rep_send.at[0, o], rep_recv.at[0, o], {"rep": peer(o)}
            )
            for o in range(1, reps)
        ]
    )
    for o, copy in enumerate(piece_copies, 1):
        copy.wait_recv()
    piece_in[0] = piece_out[...]
    total = piece_in[rep].astype(F32)
    for k in range(1, reps):
        total = total + piece_in[(rep - k + reps) % reps].astype(F32)
    whole[me] = total.astype(whole.dtype)
    whole_copies = begin(
        [to_mate(5, o, whole.at[me], whole.at[me]) for o in range(1, members)]
    )
    for copy in whole_copies:
        copy.wait_recv()
    grad_weight_ref[...] = whole[...].astype(F32).reshape(grad_weight_ref.shape)
    stores.append(store(3, grad_weight_ref, grad_weight_hbm))

    for copies in (
        edge_copies,
        scaled_copies,
        bias_copies,
        across,
        beside,
        part_copies,
        weight_copies,
        piece_copies,
        whole_copies,
    ):
        for copy in copies:
            copy.wait_send()
    for o in range(1, members):
        sum_copy(o).wait_send()
    for copy in stores:
        copy.wait()


def hand_on(*refs):
    sem = refs[8]
    copies = [pltpu.make_async_copy(refs[i], refs[4 + i], sem.at[i]) for i in range(4)]
    for copy in copies:
        copy.start()
    for copy in copies:
        copy.wait()


def per_device(
    reps, members, features, weight, bias, cotangent, degree, cols, edge_tile, edge_row, edge_col
):
    tile, width = features.shape
    depth = weight.shape[0]
    edges = edge_tile.shape[1]
    piece = depth // members
    args = (cols, features, weight, bias[None, :], cotangent, degree[None, :])
    args += (edge_tile, edge_row, edge_col)
    hbm = pl.BlockSpec(memory_space=pltpu.HBM)
    outs = (
        jax.ShapeDtypeStruct((tile, width), BF16),
        jax.ShapeDtypeStruct((tile, depth), BF16),
        jax.ShapeDtypeStruct((depth, width), F32),
        jax.ShapeDtypeStruct((1, width), F32),
    )
    results = pl.pallas_call(
        functools.partial(kernel, reps, members),
        out_shape=outs,
        in_specs=[hbm] * len(args),
        out_specs=(hbm,) * 4,
        scratch_shapes=[pltpu.SMEM(cols.shape, cols.dtype)]
        + [pltpu.VMEM(a.shape, a.dtype) for a in args[1:] + outs]
        + [
            pltpu.SemaphoreType.DMA((len(args),)),
            pltpu.SemaphoreType.DMA((4,)),
            pltpu.VMEM((2 * tile, 128), BF16),
            pltpu.VMEM((2 * tile, edges), BF16),
            pltpu.VMEM((3 * tile // 2, edges), BF16),
            pltpu.VMEM((members, 2, edges), jnp.int32),
            pltpu.VMEM((members, 3 * tile, tile), BF16),
            pltpu.VMEM((3 * tile, width), BF16),
            pltpu.VMEM((members, tile, width), BF16),
            pltpu.VMEM((members, tile, width), BF16),
            pltpu.VMEM((members, tile, width), BF16),
            pltpu.VMEM((2 * tile, width), BF16),
            pltpu.VMEM((2 * tile, width), BF16),
            pltpu.VMEM((depth, width), F32),
            pltpu.VMEM((members, piece, width), BF16),
            pltpu.VMEM((members, piece, width), BF16),
            pltpu.VMEM((piece, width), BF16),
            pltpu.VMEM((reps, piece, width), BF16),
            pltpu.VMEM((members, piece, width), BF16),
            pltpu.VMEM((8, width), F32),
            pltpu.VMEM((members, 8, width), F32),
            pltpu.VMEM((8, width), F32),
            pltpu.VMEM((reps, 8, width), F32),
            pltpu.SemaphoreType.DMA((6, members)),
            pltpu.SemaphoreType.DMA((6, members)),
            pltpu.SemaphoreType.DMA((2, reps)),
            pltpu.SemaphoreType.DMA((2, reps)),
            pltpu.SemaphoreType.DMA((4,)),
            pltpu.SemaphoreType.DMA((4,)),
        ],
        compiler_params=pltpu.CompilerParams(
            collective_id=0, has_side_effects=True, vmem_limit_bytes=LIMIT
        ),
    )(*args)
    hidden, grad_features, grad_weight, grad_bias = pl.pallas_call(
        hand_on,
        out_shape=outs,
        in_specs=[hbm] * 4,
        out_specs=(hbm,) * 4,
        scratch_shapes=[pltpu.SemaphoreType.DMA((4,))],
        compiler_params=pltpu.CompilerParams(vmem_limit_bytes=LIMIT),
    )(*results)
    return hidden, grad_features, grad_weight, grad_bias[0]


def solution(mesh):
    nodes = P(("rep", "grp"), None)
    return jax.shard_map(
        functools.partial(per_device, mesh.shape["rep"], mesh.shape["grp"]),
        mesh=mesh,
        in_specs=(nodes, P(), P(), nodes, P(("rep", "grp")), nodes, nodes, nodes, nodes),
        out_specs=(nodes, nodes, P(), P()),
        check_vma=False,
    )
```

```python
import functools

import jax
import jax.numpy as jnp
from jax import lax
from jax.experimental import pallas as pl
from jax.experimental.pallas import tpu as pltpu
from jax.sharding import PartitionSpec as P

MESH = pl.DeviceIdType.MESH
F32 = jnp.float32
BF16 = jnp.bfloat16
LIMIT = 63 * 2**20
ROWS = (((0,), (0,)), ((), ()))
LANES = (((1,), (1,)), ((), ()))


def mm(a, b, dims=(((1,), (0,)), ((), ()))):
    return lax.dot_general(a, b, dims, preferred_element_type=F32)


def kernel(
    reps,
    members,
    cols_hbm,
    features_hbm,
    weight_hbm,
    bias_hbm,
    cotangent_hbm,
    degree_hbm,
    edge_tile_hbm,
    edge_row_hbm,
    edge_col_hbm,
    hidden_hbm,
    grad_features_hbm,
    grad_weight_hbm,
    grad_bias_hbm,
    cols_ref,
    features_ref,
    weight_ref,
    bias_ref,
    cotangent_ref,
    degree_ref,
    edge_tile_ref,
    edge_row_ref,
    edge_col_ref,
    hidden_ref,
    grad_features_ref,
    grad_bias_ref,
    load_sem,
    store_sem,
    spots,
    left_hot,
    right_hot,
    listed,
    tiles_t,
    scaled,
    sums_out,
    sums,
    back,
    parts_out,
    parts,
    features_t,
    weight_out,
    weight_in,
    piece_out,
    piece_in,
    whole,
    bias_sum,
    bias_near,
    grp_send,
    grp_recv,
    rep_send,
    rep_recv,
    near_send,
    near_recv,
):
    rep = lax.axis_index("rep")
    me = lax.axis_index("grp")
    tile, width = features_ref.shape
    half = tile // 2
    edges = edge_tile_ref.shape[1]
    piece = whole.shape[1]
    chips = members // 2
    chip, core = me // 2, me % 2

    def mate(o):
        d, s = o // 2, o % 2
        return (chip + d) % chips * 2 + (core + s) % 2

    def source(o):
        d, s = o // 2, o % 2
        return (chip + chips - d) % chips * 2 + (core + s) % 2

    def reply(o):
        return (chips - o // 2) % chips * 2 + o % 2

    def peer(o):
        return (rep + o) % reps

    barrier = pltpu.get_barrier_semaphore()
    for o in range(1, members):
        pl.semaphore_signal(barrier, inc=1, device_id={"grp": mate(o)}, device_id_type=MESH)
    for o in range(1, reps):
        pl.semaphore_signal(barrier, inc=1, device_id={"rep": peer(o)}, device_id_type=MESH)
    pairs = (
        (cols_hbm, cols_ref),
        (edge_tile_hbm, edge_tile_ref),
        (edge_row_hbm, edge_row_ref),
        (edge_col_hbm, edge_col_ref),
        (features_hbm, features_ref),
        (weight_hbm, weight_ref),
        (degree_hbm, degree_ref),
        (bias_hbm, bias_ref),
        (cotangent_hbm, cotangent_ref),
    )
    loads = [
        pltpu.make_async_copy(a, b, load_sem.at[i]) for i, (a, b) in enumerate(pairs)
    ]
    for load in loads:
        load.start()

    def remote(src, dst, send, recv, to):
        return pltpu.make_async_remote_copy(
            src_ref=src,
            dst_ref=dst,
            send_sem=send,
            recv_sem=recv,
            device_id=to,
            device_id_type=MESH,
        )

    def to_mate(stage, o, src, dst):
        send, recv = grp_send.at[stage, o], grp_recv.at[stage, o]
        return remote(src, dst, send, recv, {"grp": mate(o)})

    def to_near(slot, o, src, dst):
        return remote(src, dst, near_send.at[slot], near_recv.at[slot], {"rep": peer(o)})

    def store(i, src, dst):
        copy = pltpu.make_async_copy(src, dst, store_sem.at[i])
        copy.start()
        return copy

    def begin(copies):
        for copy in copies:
            copy.start()
        return copies

    for load in loads[:4]:
        load.wait()
    edge_tile = edge_tile_ref[...]
    column = jnp.zeros_like(edge_tile)
    for t in range(cols_ref.shape[1]):
        column = jnp.where(edge_tile == t, cols_ref[0, t], column)
    listed[0, pl.ds(0, 1), :] = edge_row_ref[...]
    listed[0, pl.ds(1, 1), :] = column * tile + edge_col_ref[...]
    pl.semaphore_wait(barrier, members + reps - 2)
    edge_copies = begin(
        [to_mate(0, o, listed.at[0], listed.at[o]) for o in range(1, members)]
    )

    for load in loads[4:]:
        load.wait()
    dinv = lax.rsqrt(degree_ref[...].astype(F32))
    dinv = jnp.broadcast_to(dinv, (tile, tile)).T
    dinv = jnp.concatenate([dinv] * (width // tile), axis=1)

    own = pl.ds(tile, tile)
    scaled[own, :] = (mm(features_ref[...], weight_ref[...]) * dinv).astype(BF16)
    scaled_copies = begin(
        [
            to_near(0, 1, scaled.at[own], scaled.at[pl.ds(0, tile)]),
            to_near(1, reps - 1, scaled.at[own], scaled.at[pl.ds(2 * tile, tile)]),
        ]
    )
    features_t[...] = (
        features_ref[...].astype(F32).T.reshape(features_t.shape).astype(BF16)
    )
    spots[...] = lax.broadcasted_iota(jnp.int32, spots.shape, 0).astype(F32).astype(BF16)

    span = edges // 5 if edges % 640 == 0 else edges

    def count(o):
        row = listed[o, pl.ds(0, 1), :]
        window = listed[o, pl.ds(1, 1), :]
        column = window // tile
        part = (column >= members).astype(jnp.int32) + (column >= 2 * members).astype(jnp.int32)
        place = window - column * tile
        upper = (place >= half).astype(jnp.int32)
        left = jnp.where(column - part * members == me, upper * tile + row, -1)
        right = part * half + place - upper * half
        total = None
        for first in range(0, edges, span):
            at = pl.ds(first, span)
            for hot, key in ((left_hot, left), (right_hot, right)):
                rows = hot.shape[0]
                key = key[:, first : first + span].astype(F32)
                key = jnp.broadcast_to(key, (16, span)).astype(BF16)
                key = jnp.concatenate([key] * (rows // 16), axis=0)
                spot = jnp.concatenate([spots[:rows]] * (span // 128), axis=1)
                hot[:, at] = jnp.where(spot == key, jnp.ones_like(key), jnp.zeros_like(key))
            term = mm(right_hot[:, at], left_hot[:, at], LANES)
            total = term if total is None else total + term
        total = total.astype(BF16)
        blocks = [
            total[p * half : (p + 1) * half, u * tile : (u + 1) * tile]
            for p in range(3)
            for u in range(2)
        ]
        return jnp.concatenate(blocks, axis=0)

    counts = count(0)
    tiles_t[0] = counts
    for copy in scaled_copies:
        copy.wait_recv()
    total = mm(counts, scaled[...], ROWS)

    def sum_copy(o):
        return to_mate(1, reply(o), sums_out.at[o], sums.at[reply(o)])

    def leave(o, counts):
        sums_out[o] = mm(counts, scaled[...], ROWS).astype(BF16)
        sum_copy(o).start()

    held = None
    for o in range(1, members):
        edge_copies[o - 1].wait_recv()
        counts = count(o)
        tiles_t[o] = counts
        if held is not None:
            leave(o - 1, held)
        held = counts
    leave(members - 1, held)
    for o in range(1, members):
        to_mate(1, o, sums_out.at[o], sums.at[o]).wait_recv()
        total = total + sums[o].astype(F32)
    pre = total * dinv + bias_ref[...]
    sig = jax.nn.sigmoid(pre)
    grad_pre = cotangent_ref[...].astype(F32) * sig * (1.0 + pre * (1.0 - sig))
    back[0, pl.ds(0, tile), :] = (grad_pre * dinv).astype(BF16)
    bias_part = jnp.broadcast_to(jnp.sum(grad_pre, axis=0, keepdims=True), (8, width))
    bias_high = bias_part.astype(BF16).astype(F32)
    bias_rows = jnp.concatenate([bias_high, bias_part - bias_high], axis=0)
    back[0, pl.ds(tile, 16), :] = bias_rows.astype(BF16)
    across = [to_mate(2, o, back.at[0], back.at[o]) for o in range(2, members, 2)]
    beside = [to_mate(2, 1, back.at[0], back.at[1])]
    begin(across)
    begin(beside)
    hidden_ref[...] = (pre * sig).astype(BF16)
    stores = [store(0, hidden_ref, hidden_hbm)]

    def grad_term(o):
        return mm(tiles_t[o], back[o, pl.ds(0, tile), :])

    grads = grad_term(0)
    for d in range(1, chips):
        across[d - 1].wait_recv()
        copy = remote(
            back.at[2 * d],
            back.at[2 * d + 1],
            grp_send.at[2, 2 * d + 1],
            grp_recv.at[2, 2 * d + 1],
            {"grp": mate(1)},
        )
        copy.start()
        beside.append(copy)
        grads = grads + grad_term(2 * d)
    for d in range(chips):
        beside[d].wait_recv()
        grads = grads + grad_term(2 * d + 1)
    parts_out[pl.ds(0, tile), :] = grads[:tile].astype(BF16)
    parts_out[pl.ds(tile, tile), :] = grads[2 * tile :].astype(BF16)
    lower, upper = pl.ds(0, tile), pl.ds(tile, tile)
    part_copies = begin(
        [
            to_near(2, reps - 1, parts_out.at[lower], parts.at[lower]),
            to_near(3, 1, parts_out.at[upper], parts.at[upper]),
        ]
    )
    bias_rows = jnp.zeros((16, width), F32)
    for o in range(members):
        bias_rows = bias_rows + back[o, pl.ds(tile, 16), :].astype(F32)
    bias_total = bias_rows[:8] + bias_rows[8:]
    bias_sum[...] = bias_total
    bias_copies = begin(
        [
            remote(bias_sum, bias_near.at[o], rep_send.at[1, o], rep_recv.at[1, o], {"rep": peer(o)})
            for o in range(1, reps)
        ]
    )
    for copy in part_copies:
        copy.wait_recv()
    grad_sum = grads[tile : 2 * tile] + parts[lower, :].astype(F32) + parts[upper, :].astype(F32)
    grad_scaled = (grad_sum * dinv).astype(BF16)

    weight_copies = []
    for o in list(range(1, members)) + [0]:
        block = mm(features_t[mate(o)], grad_scaled)
        if o == 0:
            total = block
        else:
            weight_out[o] = block.astype(BF16)
            weight_copies += begin([to_mate(4, o, weight_out.at[o], weight_in.at[o])])
    grad_features_ref[...] = mm(grad_scaled, weight_ref[...], LANES).astype(BF16)
    stores.append(store(1, grad_features_ref, grad_features_hbm))
    for o, copy in enumerate(bias_copies, 1):
        copy.wait_recv()
        bias_total = bias_total + bias_near[o]
    grad_bias_ref[...] = bias_total[:1]
    stores.append(store(2, grad_bias_ref, grad_bias_hbm))
    for o, copy in enumerate(weight_copies, 1):
        copy.wait_recv()
        total = total + weight_in[o].astype(F32)
    piece_out[...] = total.astype(BF16)
    piece_copies = begin(
        [
            remote(
                piece_out, piece_in.at[o], rep_send.at[0, o], rep_recv.at[0, o], {"rep": peer(o)}
            )
            for o in range(1, reps)
        ]
    )
    for o, copy in enumerate(piece_copies, 1):
        copy.wait_recv()
    piece_in[0] = piece_out[...]
    total = piece_in[rep].astype(F32)
    for k in range(1, reps):
        total = total + piece_in[(rep - k + reps) % reps].astype(F32)
    whole[me] = total.astype(whole.dtype)
    whole_copies = begin(
        [to_mate(5, o, whole.at[me], whole.at[me]) for o in range(1, members)]
    )
    for copy in whole_copies:
        copy.wait_recv()
    stores.append(store(3, whole, grad_weight_hbm))

    for copies in (
        edge_copies,
        scaled_copies,
        bias_copies,
        across,
        beside,
        part_copies,
        weight_copies,
        piece_copies,
        whole_copies,
    ):
        for copy in copies:
            copy.wait_send()
    for o in range(1, members):
        sum_copy(o).wait_send()
    for copy in stores:
        copy.wait()


def hand_on(*refs):
    given, results, held, load_sem, store_sem = refs[:4], refs[4:8], refs[8:13], refs[13], refs[14]
    loads = [pltpu.make_async_copy(given[i], held[i], load_sem.at[i]) for i in range(4)]
    for load in loads:
        load.start()
    stores = []
    for i in (3, 0, 1, 2):
        loads[i].wait()
        source = held[i]
        if i == 2:
            source = held[4]
            source[...] = held[2][...].astype(F32).reshape(source.shape)
        stores.append(pltpu.make_async_copy(source, results[i], store_sem.at[i]))
        stores[-1].start()
    for copy in stores:
        copy.wait()


def per_device(
    reps, members, features, weight, bias, cotangent, degree, cols, edge_tile, edge_row, edge_col
):
    tile, width = features.shape
    depth = weight.shape[0]
    edges = edge_tile.shape[1]
    piece = depth // members
    args = (cols, features, weight, bias[None, :], cotangent, degree[None, :])
    args += (edge_tile, edge_row, edge_col)
    hbm = pl.BlockSpec(memory_space=pltpu.HBM)
    outs = (
        jax.ShapeDtypeStruct((tile, width), BF16),
        jax.ShapeDtypeStruct((tile, depth), BF16),
        jax.ShapeDtypeStruct((depth, width), F32),
        jax.ShapeDtypeStruct((1, width), F32),
    )
    given = outs[:2] + (jax.ShapeDtypeStruct((members, piece, width), BF16),) + outs[3:]
    results = pl.pallas_call(
        functools.partial(kernel, reps, members),
        out_shape=given,
        in_specs=[hbm] * len(args),
        out_specs=(hbm,) * 4,
        scratch_shapes=[pltpu.SMEM(cols.shape, cols.dtype)]
        + [pltpu.VMEM(a.shape, a.dtype) for a in args[1:] + outs[:2] + outs[3:]]
        + [
            pltpu.SemaphoreType.DMA((len(args),)),
            pltpu.SemaphoreType.DMA((4,)),
            pltpu.VMEM((2 * tile, 128), BF16),
            pltpu.VMEM((2 * tile, edges), BF16),
            pltpu.VMEM((3 * tile // 2, edges), BF16),
            pltpu.VMEM((members, 2, edges), jnp.int32),
            pltpu.VMEM((members, 3 * tile, tile), BF16),
            pltpu.VMEM((3 * tile, width), BF16),
            pltpu.VMEM((members, tile, width), BF16),
            pltpu.VMEM((members, tile, width), BF16),
            pltpu.VMEM((members, tile + 16, width), BF16),
            pltpu.VMEM((2 * tile, width), BF16),
            pltpu.VMEM((2 * tile, width), BF16),
            pltpu.VMEM((members, piece, tile), BF16),
            pltpu.VMEM((members, piece, width), BF16),
            pltpu.VMEM((members, piece, width), BF16),
            pltpu.VMEM((piece, width), BF16),
            pltpu.VMEM((reps, piece, width), BF16),
            pltpu.VMEM((members, piece, width), BF16),
            pltpu.VMEM((8, width), F32),
            pltpu.VMEM((reps, 8, width), F32),
            pltpu.SemaphoreType.DMA((6, members)),
            pltpu.SemaphoreType.DMA((6, members)),
            pltpu.SemaphoreType.DMA((2, reps)),
            pltpu.SemaphoreType.DMA((2, reps)),
            pltpu.SemaphoreType.DMA((4,)),
            pltpu.SemaphoreType.DMA((4,)),
        ],
        compiler_params=pltpu.CompilerParams(
            collective_id=0, has_side_effects=True, vmem_limit_bytes=LIMIT
        ),
    )(*args)
    hidden, grad_features, grad_weight, grad_bias = pl.pallas_call(
        hand_on,
        out_shape=outs,
        in_specs=[hbm] * 4,
        out_specs=(hbm,) * 4,
        scratch_shapes=[pltpu.VMEM(a.shape, a.dtype) for a in given + outs[2:3]]
        + [pltpu.SemaphoreType.DMA((4,)), pltpu.SemaphoreType.DMA((4,))],
        compiler_params=pltpu.CompilerParams(vmem_limit_bytes=LIMIT),
    )(*results)
    return hidden, grad_features, grad_weight, grad_bias[0]


def solution(mesh):
    nodes = P(("rep", "grp"), None)
    return jax.shard_map(
        functools.partial(per_device, mesh.shape["rep"], mesh.shape["grp"]),
        mesh=mesh,
        in_specs=(nodes, P(), P(), nodes, P(("rep", "grp")), nodes, nodes, nodes, nodes),
        out_specs=(nodes, nodes, P(), P()),
        check_vma=False,
    )
```

```python
import functools

import jax
import jax.numpy as jnp
from jax import lax
from jax.experimental import pallas as pl
from jax.experimental.pallas import tpu as pltpu
from jax.sharding import PartitionSpec as P

MESH = pl.DeviceIdType.MESH
F32 = jnp.float32
BF16 = jnp.bfloat16
LIMIT = 63 * 2**20
ROWS = (((0,), (0,)), ((), ()))
LANES = (((1,), (1,)), ((), ()))


def mm(a, b, dims=(((1,), (0,)), ((), ()))):
    return lax.dot_general(a, b, dims, preferred_element_type=F32)


def kernel(
    reps,
    members,
    cols_hbm,
    features_hbm,
    weight_hbm,
    bias_hbm,
    cotangent_hbm,
    degree_hbm,
    edge_tile_hbm,
    edge_row_hbm,
    edge_col_hbm,
    hidden_hbm,
    grad_features_hbm,
    grad_weight_hbm,
    grad_bias_hbm,
    cols_ref,
    features_ref,
    weight_ref,
    bias_ref,
    cotangent_ref,
    degree_ref,
    edge_tile_ref,
    edge_row_ref,
    edge_col_ref,
    hidden_ref,
    grad_features_ref,
    grad_bias_ref,
    load_sem,
    store_sem,
    spots,
    left_hot,
    right_hot,
    listed,
    tiles_t,
    scaled,
    sums_out,
    sums,
    own_sum,
    grads,
    back,
    parts_out,
    parts,
    features_t,
    weight_out,
    weight_in,
    piece_out,
    piece_in,
    whole,
    bias_sum,
    bias_near,
    grp_send,
    grp_recv,
    rep_send,
    rep_recv,
    near_send,
    near_recv,
):
    rep = lax.axis_index("rep")
    me = lax.axis_index("grp")
    tile, width = features_ref.shape
    half = tile // 2
    edges = edge_tile_ref.shape[1]
    piece = whole.shape[1]
    chips = members // 2
    chip, core = me // 2, me % 2

    def mate(o):
        d, s = o // 2, o % 2
        return (chip + d) % chips * 2 + (core + s) % 2

    def source(o):
        d, s = o // 2, o % 2
        return (chip + chips - d) % chips * 2 + (core + s) % 2

    def reply(o):
        return (chips - o // 2) % chips * 2 + o % 2

    def peer(o):
        return (rep + o) % reps

    barrier = pltpu.get_barrier_semaphore()
    for o in range(1, members):
        pl.semaphore_signal(barrier, inc=1, device_id={"grp": mate(o)}, device_id_type=MESH)
    for o in range(1, reps):
        pl.semaphore_signal(barrier, inc=1, device_id={"rep": peer(o)}, device_id_type=MESH)
    pairs = (
        (cols_hbm, cols_ref),
        (edge_tile_hbm, edge_tile_ref),
        (edge_row_hbm, edge_row_ref),
        (edge_col_hbm, edge_col_ref),
        (features_hbm, features_ref),
        (weight_hbm, weight_ref),
        (degree_hbm, degree_ref),
        (bias_hbm, bias_ref),
        (cotangent_hbm, cotangent_ref),
    )
    loads = [
        pltpu.make_async_copy(a, b, load_sem.at[i]) for i, (a, b) in enumerate(pairs)
    ]
    for load in loads:
        load.start()

    def remote(src, dst, send, recv, to):
        return pltpu.make_async_remote_copy(
            src_ref=src,
            dst_ref=dst,
            send_sem=send,
            recv_sem=recv,
            device_id=to,
            device_id_type=MESH,
        )

    def to_mate(stage, o, src, dst):
        send, recv = grp_send.at[stage, o], grp_recv.at[stage, o]
        return remote(src, dst, send, recv, {"grp": mate(o)})

    def to_near(slot, o, src, dst):
        return remote(src, dst, near_send.at[slot], near_recv.at[slot], {"rep": peer(o)})

    def store(i, src, dst):
        copy = pltpu.make_async_copy(src, dst, store_sem.at[i])
        copy.start()
        return copy

    def each(first, last, act):
        def body(i, _):
            act(i)
            return 0

        lax.fori_loop(first, last, body, 0)

    def begin(copies):
        for copy in copies:
            copy.start()
        return copies

    for load in loads[:4]:
        load.wait()
    edge_tile = edge_tile_ref[...]
    column = jnp.zeros_like(edge_tile)
    for t in range(cols_ref.shape[1]):
        column = jnp.where(edge_tile == t, cols_ref[0, t], column)
    listed[0, pl.ds(0, 1), :] = edge_row_ref[...]
    listed[0, pl.ds(1, 1), :] = column * tile + edge_col_ref[...]
    pl.semaphore_wait(barrier, members + reps - 2)

    def edge_copy(o):
        return to_mate(0, o, listed.at[0], listed.at[o])

    each(1, members, lambda o: edge_copy(o).start())

    for load in loads[4:]:
        load.wait()
    dinv = lax.rsqrt(degree_ref[...].astype(F32))
    dinv = jnp.broadcast_to(dinv, (tile, tile)).T
    dinv = jnp.concatenate([dinv] * (width // tile), axis=1)

    own = pl.ds(tile, tile)
    scaled[own, :] = (mm(features_ref[...], weight_ref[...]) * dinv).astype(BF16)
    scaled_copies = begin(
        [
            to_near(0, 1, scaled.at[own], scaled.at[pl.ds(0, tile)]),
            to_near(1, reps - 1, scaled.at[own], scaled.at[pl.ds(2 * tile, tile)]),
        ]
    )
    features_t[...] = (
        features_ref[...].astype(F32).T.reshape(features_t.shape).astype(BF16)
    )
    spots[...] = lax.broadcasted_iota(jnp.int32, spots.shape, 0).astype(F32).astype(BF16)

    span = edges // 5 if edges % 640 == 0 else edges

    def count(o):
        row = listed[o, pl.ds(0, 1), :]
        window = listed[o, pl.ds(1, 1), :]
        column = window // tile
        part = (column >= members).astype(jnp.int32) + (column >= 2 * members).astype(jnp.int32)
        place = window - column * tile
        upper = (place >= half).astype(jnp.int32)
        left = jnp.where(column - part * members == me, upper * tile + row, -1)
        right = part * half + place - upper * half
        total = None
        for first in range(0, edges, span):
            at = pl.ds(first, span)
            for hot, key in ((left_hot, left), (right_hot, right)):
                rows = hot.shape[0]
                key = key[:, first : first + span].astype(F32)
                key = jnp.broadcast_to(key, (16, span)).astype(BF16)
                key = jnp.concatenate([key] * (rows // 16), axis=0)
                spot = jnp.concatenate([spots[:rows]] * (span // 128), axis=1)
                hot[:, at] = jnp.where(spot == key, jnp.ones_like(key), jnp.zeros_like(key))
            term = mm(right_hot[:, at], left_hot[:, at], LANES)
            total = term if total is None else total + term
        total = total.astype(BF16)
        blocks = [
            total[p * half : (p + 1) * half, u * tile : (u + 1) * tile]
            for p in range(3)
            for u in range(2)
        ]
        return jnp.concatenate(blocks, axis=0)

    def sum_copy(o):
        return to_mate(1, reply(o), sums_out.at[o], sums.at[reply(o)])

    def forward(o):
        @pl.when(o > 0)
        def _():
            edge_copy(o).wait_recv()

        tiles_t[o] = count(o)

        @pl.when(o == 0)
        def _():
            for copy in scaled_copies:
                copy.wait_recv()

        term = mm(tiles_t[o], scaled[...], ROWS)

        @pl.when(o == 0)
        def _():
            own_sum[...] = term

        @pl.when(o > 0)
        def _():
            sums_out[o] = term.astype(BF16)
            sum_copy(o).start()

    each(0, members, forward)

    def add_sum(o, total):
        to_mate(1, o, sums_out.at[o], sums.at[o]).wait_recv()
        return total + sums[o].astype(F32)

    total = lax.fori_loop(1, members, add_sum, own_sum[...])
    pre = total * dinv + bias_ref[...]
    sig = jax.nn.sigmoid(pre)
    grad_pre = cotangent_ref[...].astype(F32) * sig * (1.0 + pre * (1.0 - sig))
    back[0, pl.ds(0, tile), :] = (grad_pre * dinv).astype(BF16)
    bias_part = jnp.broadcast_to(jnp.sum(grad_pre, axis=0, keepdims=True), (8, width))
    bias_high = bias_part.astype(BF16).astype(F32)
    bias_rows = jnp.concatenate([bias_high, bias_part - bias_high], axis=0)
    back[0, pl.ds(tile, 16), :] = bias_rows.astype(BF16)
    def back_copy(o):
        return to_mate(2, o, back.at[0], back.at[o])

    def relay(d):
        send, recv = grp_send.at[2, 2 * d + 1], grp_recv.at[2, 2 * d + 1]
        return remote(back.at[2 * d], back.at[2 * d + 1], send, recv, {"grp": mate(1)})

    each(1, chips, lambda d: back_copy(2 * d).start())
    back_copy(1).start()
    hidden_ref[...] = (pre * sig).astype(BF16)
    stores = [store(0, hidden_ref, hidden_hbm)]

    def grad_term(o):
        return mm(tiles_t[o], back[o, pl.ds(0, tile), :])

    grads[...] = grad_term(0)

    def grad_across(d):
        back_copy(2 * d).wait_recv()
        relay(d).start()
        grads[...] += grad_term(2 * d)

    def grad_beside(d):
        relay(d).wait_recv()
        grads[...] += grad_term(2 * d + 1)

    each(1, chips, grad_across)
    each(0, chips, grad_beside)
    parts_out[pl.ds(0, tile), :] = grads[:tile, :].astype(BF16)
    parts_out[pl.ds(tile, tile), :] = grads[2 * tile :, :].astype(BF16)
    lower, upper = pl.ds(0, tile), pl.ds(tile, tile)
    part_copies = begin(
        [
            to_near(2, reps - 1, parts_out.at[lower], parts.at[lower]),
            to_near(3, 1, parts_out.at[upper], parts.at[upper]),
        ]
    )
    bias_rows = jnp.zeros((16, width), F32)
    for o in range(members):
        bias_rows = bias_rows + back[o, pl.ds(tile, 16), :].astype(F32)
    bias_total = bias_rows[:8] + bias_rows[8:]
    bias_sum[...] = bias_total
    bias_copies = begin(
        [
            remote(bias_sum, bias_near.at[o], rep_send.at[1, o], rep_recv.at[1, o], {"rep": peer(o)})
            for o in range(1, reps)
        ]
    )
    for copy in part_copies:
        copy.wait_recv()
    grad_sum = grads[tile : 2 * tile, :] + parts[lower, :].astype(F32) + parts[upper, :].astype(F32)
    grad_scaled = (grad_sum * dinv).astype(BF16)

    def weight_copy(o):
        return to_mate(3, o, weight_out.at[o], weight_in.at[o])

    def weight_piece(o):
        weight_out[o] = mm(features_t[mate(o)], grad_scaled).astype(BF16)
        weight_copy(o).start()

    each(1, members, weight_piece)
    total = mm(features_t[me], grad_scaled)
    grad_features_ref[...] = mm(grad_scaled, weight_ref[...], LANES).astype(BF16)
    stores.append(store(1, grad_features_ref, grad_features_hbm))
    for o, copy in enumerate(bias_copies, 1):
        copy.wait_recv()
        bias_total = bias_total + bias_near[o]
    grad_bias_ref[...] = bias_total[:1]
    stores.append(store(2, grad_bias_ref, grad_bias_hbm))

    def add_piece(o, total):
        weight_copy(o).wait_recv()
        return total + weight_in[o].astype(F32)

    total = lax.fori_loop(1, members, add_piece, total)
    piece_out[...] = total.astype(BF16)
    piece_copies = begin(
        [
            remote(
                piece_out, piece_in.at[o], rep_send.at[0, o], rep_recv.at[0, o], {"rep": peer(o)}
            )
            for o in range(1, reps)
        ]
    )
    for o, copy in enumerate(piece_copies, 1):
        copy.wait_recv()
    piece_in[0] = piece_out[...]
    total = piece_in[rep].astype(F32)
    for k in range(1, reps):
        total = total + piece_in[(rep - k + reps) % reps].astype(F32)
    whole[me] = total.astype(whole.dtype)

    def whole_copy(o):
        return to_mate(4, o, whole.at[me], whole.at[me])

    each(1, members, lambda o: whole_copy(o).start())
    each(1, members, lambda o: whole_copy(o).wait_recv())
    stores.append(store(3, whole, grad_weight_hbm))

    for copies in (scaled_copies, bias_copies, part_copies, piece_copies):
        for copy in copies:
            copy.wait_send()

    def sent(o):
        for copy in (edge_copy(o), sum_copy(o), weight_copy(o), whole_copy(o)):
            copy.wait_send()

    each(1, members, sent)
    each(1, chips, lambda d: back_copy(2 * d).wait_send())
    each(0, chips, lambda d: relay(d).wait_send())
    for copy in stores:
        copy.wait()


def hand_on(*refs):
    given, results, held, load_sem, store_sem = refs[:4], refs[4:8], refs[8:13], refs[13], refs[14]
    loads = [pltpu.make_async_copy(given[i], held[i], load_sem.at[i]) for i in range(4)]
    for load in loads:
        load.start()
    stores = []
    for i in (3, 0, 1, 2):
        loads[i].wait()
        source = held[i]
        if i == 2:
            source = held[4]
            source[...] = held[2][...].astype(F32).reshape(source.shape)
        stores.append(pltpu.make_async_copy(source, results[i], store_sem.at[i]))
        stores[-1].start()
    for copy in stores:
        copy.wait()


def per_device(
    reps, members, features, weight, bias, cotangent, degree, cols, edge_tile, edge_row, edge_col
):
    tile, width = features.shape
    depth = weight.shape[0]
    edges = edge_tile.shape[1]
    piece = depth // members
    args = (cols, features, weight, bias[None, :], cotangent, degree[None, :])
    args += (edge_tile, edge_row, edge_col)
    hbm = pl.BlockSpec(memory_space=pltpu.HBM)
    outs = (
        jax.ShapeDtypeStruct((tile, width), BF16),
        jax.ShapeDtypeStruct((tile, depth), BF16),
        jax.ShapeDtypeStruct((depth, width), F32),
        jax.ShapeDtypeStruct((1, width), F32),
    )
    given = outs[:2] + (jax.ShapeDtypeStruct((members, piece, width), BF16),) + outs[3:]
    results = pl.pallas_call(
        functools.partial(kernel, reps, members),
        out_shape=given,
        in_specs=[hbm] * len(args),
        out_specs=(hbm,) * 4,
        scratch_shapes=[pltpu.SMEM(cols.shape, cols.dtype)]
        + [pltpu.VMEM(a.shape, a.dtype) for a in args[1:] + outs[:2] + outs[3:]]
        + [
            pltpu.SemaphoreType.DMA((len(args),)),
            pltpu.SemaphoreType.DMA((4,)),
            pltpu.VMEM((2 * tile, 128), BF16),
            pltpu.VMEM((2 * tile, edges), BF16),
            pltpu.VMEM((3 * tile // 2, edges), BF16),
            pltpu.VMEM((members, 2, edges), jnp.int32),
            pltpu.VMEM((members, 3 * tile, tile), BF16),
            pltpu.VMEM((3 * tile, width), BF16),
            pltpu.VMEM((members, tile, width), BF16),
            pltpu.VMEM((members, tile, width), BF16),
            pltpu.VMEM((tile, width), F32),
            pltpu.VMEM((3 * tile, width), F32),
            pltpu.VMEM((members, tile + 16, width), BF16),
            pltpu.VMEM((2 * tile, width), BF16),
            pltpu.VMEM((2 * tile, width), BF16),
            pltpu.VMEM((members, piece, tile), BF16),
            pltpu.VMEM((members, piece, width), BF16),
            pltpu.VMEM((members, piece, width), BF16),
            pltpu.VMEM((piece, width), BF16),
            pltpu.VMEM((reps, piece, width), BF16),
            pltpu.VMEM((members, piece, width), BF16),
            pltpu.VMEM((8, width), F32),
            pltpu.VMEM((reps, 8, width), F32),
            pltpu.SemaphoreType.DMA((5, members)),
            pltpu.SemaphoreType.DMA((5, members)),
            pltpu.SemaphoreType.DMA((2, reps)),
            pltpu.SemaphoreType.DMA((2, reps)),
            pltpu.SemaphoreType.DMA((4,)),
            pltpu.SemaphoreType.DMA((4,)),
        ],
        compiler_params=pltpu.CompilerParams(
            collective_id=0, has_side_effects=True, vmem_limit_bytes=LIMIT
        ),
    )(*args)
    hidden, grad_features, grad_weight, grad_bias = pl.pallas_call(
        hand_on,
        out_shape=outs,
        in_specs=[hbm] * 4,
        out_specs=(hbm,) * 4,
        scratch_shapes=[pltpu.VMEM(a.shape, a.dtype) for a in given + outs[2:3]]
        + [pltpu.SemaphoreType.DMA((4,)), pltpu.SemaphoreType.DMA((4,))],
        compiler_params=pltpu.CompilerParams(vmem_limit_bytes=LIMIT),
    )(*results)
    return hidden, grad_features, grad_weight, grad_bias[0]


def solution(mesh):
    nodes = P(("rep", "grp"), None)
    return jax.shard_map(
        functools.partial(per_device, mesh.shape["rep"], mesh.shape["grp"]),
        mesh=mesh,
        in_specs=(nodes, P(), P(), nodes, P(("rep", "grp")), nodes, nodes, nodes, nodes),
        out_specs=(nodes, nodes, P(), P()),
        check_vma=False,
    )
```

```python
import functools

import jax
import jax.numpy as jnp
from jax import lax
from jax.experimental import pallas as pl
from jax.experimental.pallas import tpu as pltpu
from jax.sharding import PartitionSpec as P

MESH = pl.DeviceIdType.MESH
F32 = jnp.float32
BF16 = jnp.bfloat16
LIMIT = 63 * 2**20
ROWS = (((0,), (0,)), ((), ()))
LANES = (((1,), (1,)), ((), ()))


def mm(a, b, dims=(((1,), (0,)), ((), ()))):
    return lax.dot_general(a, b, dims, preferred_element_type=F32)


def kernel(
    reps,
    members,
    cols_hbm,
    features_hbm,
    weight_hbm,
    bias_hbm,
    cotangent_hbm,
    degree_hbm,
    edge_tile_hbm,
    edge_row_hbm,
    edge_col_hbm,
    hidden_hbm,
    grad_features_hbm,
    grad_weight_hbm,
    grad_bias_hbm,
    cols_ref,
    features_ref,
    weight_ref,
    bias_ref,
    cotangent_ref,
    degree_ref,
    edge_tile_ref,
    edge_row_ref,
    edge_col_ref,
    hidden_ref,
    grad_features_ref,
    grad_bias_ref,
    load_sem,
    store_sem,
    spots,
    left_hot,
    right_hot,
    listed,
    tiles_t,
    scaled,
    sums_out,
    sums,
    own_sum,
    grads,
    back,
    parts_out,
    parts,
    features_t,
    weight_out,
    weight_in,
    piece_out,
    piece_in,
    whole,
    bias_sum,
    bias_near,
    grp_send,
    grp_recv,
    rep_send,
    rep_recv,
    near_send,
    near_recv,
):
    rep = lax.axis_index("rep")
    me = lax.axis_index("grp")
    tile, width = features_ref.shape
    middle = 3 * tile // 2
    edges = edge_tile_ref.shape[1]
    piece = whole.shape[1]
    chips = members // 2
    chip, core = me // 2, me % 2

    def mate(o):
        d, s = o // 2, o % 2
        return (chip + d) % chips * 2 + (core + s) % 2

    def source(o):
        d, s = o // 2, o % 2
        return (chip + chips - d) % chips * 2 + (core + s) % 2

    def reply(o):
        return (chips - o // 2) % chips * 2 + o % 2

    def peer(o):
        return (rep + o) % reps

    barrier = pltpu.get_barrier_semaphore()
    for o in range(1, members):
        pl.semaphore_signal(barrier, inc=1, device_id={"grp": mate(o)}, device_id_type=MESH)
    for o in range(1, reps):
        pl.semaphore_signal(barrier, inc=1, device_id={"rep": peer(o)}, device_id_type=MESH)
    pairs = (
        (cols_hbm, cols_ref),
        (edge_tile_hbm, edge_tile_ref),
        (edge_row_hbm, edge_row_ref),
        (edge_col_hbm, edge_col_ref),
        (features_hbm, features_ref),
        (weight_hbm, weight_ref),
        (degree_hbm, degree_ref),
        (bias_hbm, bias_ref),
        (cotangent_hbm, cotangent_ref),
    )
    loads = [
        pltpu.make_async_copy(a, b, load_sem.at[i]) for i, (a, b) in enumerate(pairs)
    ]
    for load in loads:
        load.start()

    def remote(src, dst, send, recv, to):
        return pltpu.make_async_remote_copy(
            src_ref=src,
            dst_ref=dst,
            send_sem=send,
            recv_sem=recv,
            device_id=to,
            device_id_type=MESH,
        )

    def to_mate(stage, o, src, dst):
        send, recv = grp_send.at[stage, o], grp_recv.at[stage, o]
        return remote(src, dst, send, recv, {"grp": mate(o)})

    def to_near(slot, o, src, dst):
        return remote(src, dst, near_send.at[slot], near_recv.at[slot], {"rep": peer(o)})

    def store(i, src, dst):
        copy = pltpu.make_async_copy(src, dst, store_sem.at[i])
        copy.start()
        return copy

    def each(first, last, act):
        def body(i, _):
            act(i)
            return 0

        lax.fori_loop(first, last, body, 0)

    def begin(copies):
        for copy in copies:
            copy.start()
        return copies

    for load in loads[:4]:
        load.wait()
    edge_tile = edge_tile_ref[...]
    column = jnp.zeros_like(edge_tile)
    for t in range(cols_ref.shape[1]):
        column = jnp.where(edge_tile == t, cols_ref[0, t], column)
    listed[0, pl.ds(0, 1), :] = edge_row_ref[...]
    listed[0, pl.ds(1, 1), :] = column * tile + edge_col_ref[...]
    pl.semaphore_wait(barrier, members + reps - 2)

    def edge_copy(o):
        return to_mate(0, o, listed.at[0], listed.at[o])

    each(1, members, lambda o: edge_copy(o).start())

    for load in loads[4:]:
        load.wait()
    dinv = lax.rsqrt(degree_ref[...].astype(F32))
    dinv = jnp.broadcast_to(dinv, (tile, tile)).T
    dinv = jnp.concatenate([dinv] * (width // tile), axis=1)

    own = pl.ds(tile, tile)
    scaled[own, :] = (mm(features_ref[...], weight_ref[...]) * dinv).astype(BF16)
    scaled_copies = begin(
        [
            to_near(0, 1, scaled.at[own], scaled.at[pl.ds(0, tile)]),
            to_near(1, reps - 1, scaled.at[own], scaled.at[pl.ds(2 * tile, tile)]),
        ]
    )
    features_t[...] = (
        features_ref[...].astype(F32).T.reshape(features_t.shape).astype(BF16)
    )
    spot = lax.broadcasted_iota(jnp.int32, spots.shape, 0) - middle
    spots[...] = spot.astype(F32).astype(BF16)

    span = edges // 5 if edges % 640 == 0 else edges

    def count(o):
        row = listed[o, pl.ds(0, 1), :]
        window = listed[o, pl.ds(1, 1), :]
        column = window // tile
        part = (column >= members).astype(jnp.int32) + (column >= 2 * members).astype(jnp.int32)
        place = window - column * tile
        left = jnp.where(column - part * members == me, row, -1)
        right = part * tile + place - middle
        total = None
        for first in range(0, edges, span):
            at = pl.ds(first, span)
            for hot, key, low in ((left_hot, left, middle), (right_hot, right, 0)):
                rows = hot.shape[0]
                key = key[:, first : first + span].astype(F32)
                key = jnp.broadcast_to(key, (16, span)).astype(BF16)
                key = jnp.concatenate([key] * (rows // 16), axis=0)
                spot = jnp.concatenate([spots[low : low + rows]] * (span // 128), axis=1)
                hot[:, at] = jnp.where(spot == key, jnp.ones_like(key), jnp.zeros_like(key))
            term = mm(right_hot[:, at], left_hot[:, at], LANES)
            total = term if total is None else total + term
        return total.astype(BF16)

    def sum_copy(o):
        return to_mate(1, reply(o), sums_out.at[o], sums.at[reply(o)])

    def forward(o):
        @pl.when(o > 0)
        def _():
            edge_copy(o).wait_recv()

        tiles_t[o] = count(o)

        @pl.when(o == 0)
        def _():
            for copy in scaled_copies:
                copy.wait_recv()

        term = mm(tiles_t[o], scaled[...], ROWS)

        @pl.when(o == 0)
        def _():
            own_sum[...] = term

        @pl.when(o > 0)
        def _():
            sums_out[o] = term.astype(BF16)
            sum_copy(o).start()

    each(0, members, forward)

    def add_sum(o, total):
        to_mate(1, o, sums_out.at[o], sums.at[o]).wait_recv()
        return total + sums[o].astype(F32)

    total = lax.fori_loop(1, members, add_sum, own_sum[...])
    pre = total * dinv + bias_ref[...]
    sig = jax.nn.sigmoid(pre)
    grad_pre = cotangent_ref[...].astype(F32) * sig * (1.0 + pre * (1.0 - sig))
    back[0, pl.ds(0, tile), :] = (grad_pre * dinv).astype(BF16)
    bias_part = jnp.broadcast_to(jnp.sum(grad_pre, axis=0, keepdims=True), (8, width))
    bias_high = bias_part.astype(BF16).astype(F32)
    bias_rows = jnp.concatenate([bias_high, bias_part - bias_high], axis=0)
    back[0, pl.ds(tile, 16), :] = bias_rows.astype(BF16)
    def back_copy(o):
        return to_mate(2, o, back.at[0], back.at[o])

    def relay(d):
        send, recv = grp_send.at[2, 2 * d + 1], grp_recv.at[2, 2 * d + 1]
        return remote(back.at[2 * d], back.at[2 * d + 1], send, recv, {"grp": mate(1)})

    each(1, chips, lambda d: back_copy(2 * d).start())
    back_copy(1).start()
    hidden_ref[...] = (pre * sig).astype(BF16)
    stores = [store(0, hidden_ref, hidden_hbm)]

    def grad_term(o):
        return mm(tiles_t[o], back[o, pl.ds(0, tile), :])

    grads[...] = grad_term(0)

    def grad_across(d):
        back_copy(2 * d).wait_recv()
        relay(d).start()
        grads[...] += grad_term(2 * d)

    def grad_beside(d):
        relay(d).wait_recv()
        grads[...] += grad_term(2 * d + 1)

    each(1, chips, grad_across)
    each(0, chips, grad_beside)
    parts_out[pl.ds(0, tile), :] = grads[:tile, :].astype(BF16)
    parts_out[pl.ds(tile, tile), :] = grads[2 * tile :, :].astype(BF16)
    lower, upper = pl.ds(0, tile), pl.ds(tile, tile)
    part_copies = begin(
        [
            to_near(2, reps - 1, parts_out.at[lower], parts.at[lower]),
            to_near(3, 1, parts_out.at[upper], parts.at[upper]),
        ]
    )
    bias_rows = jnp.zeros((16, width), F32)
    for o in range(members):
        bias_rows = bias_rows + back[o, pl.ds(tile, 16), :].astype(F32)
    bias_total = bias_rows[:8] + bias_rows[8:]
    bias_sum[...] = bias_total
    bias_copies = begin(
        [
            remote(bias_sum, bias_near.at[o], rep_send.at[1, o], rep_recv.at[1, o], {"rep": peer(o)})
            for o in range(1, reps)
        ]
    )
    for copy in part_copies:
        copy.wait_recv()
    grad_sum = grads[tile : 2 * tile, :] + parts[lower, :].astype(F32) + parts[upper, :].astype(F32)
    grad_scaled = (grad_sum * dinv).astype(BF16)

    def weight_copy(o):
        return to_mate(3, o, weight_out.at[o], weight_in.at[o])

    def weight_piece(o):
        weight_out[o] = mm(features_t[mate(o)], grad_scaled).astype(BF16)
        weight_copy(o).start()

    each(1, members, weight_piece)
    total = mm(features_t[me], grad_scaled)
    grad_features_ref[...] = mm(grad_scaled, weight_ref[...], LANES).astype(BF16)
    stores.append(store(1, grad_features_ref, grad_features_hbm))
    for o, copy in enumerate(bias_copies, 1):
        copy.wait_recv()
        bias_total = bias_total + bias_near[o]
    grad_bias_ref[...] = bias_total[:1]
    stores.append(store(2, grad_bias_ref, grad_bias_hbm))

    def add_piece(o, total):
        weight_copy(o).wait_recv()
        return total + weight_in[o].astype(F32)

    total = lax.fori_loop(1, members, add_piece, total)
    piece_out[...] = total.astype(BF16)
    piece_copies = begin(
        [
            remote(
                piece_out, piece_in.at[o], rep_send.at[0, o], rep_recv.at[0, o], {"rep": peer(o)}
            )
            for o in range(1, reps)
        ]
    )
    for o, copy in enumerate(piece_copies, 1):
        copy.wait_recv()
    piece_in[0] = piece_out[...]
    total = piece_in[rep].astype(F32)
    for k in range(1, reps):
        total = total + piece_in[(rep - k + reps) % reps].astype(F32)
    whole[me] = total.astype(whole.dtype)

    def whole_copy(o):
        return to_mate(4, o, whole.at[me], whole.at[me])

    each(1, members, lambda o: whole_copy(o).start())
    each(1, members, lambda o: whole_copy(o).wait_recv())
    stores.append(store(3, whole, grad_weight_hbm))

    for copies in (scaled_copies, bias_copies, part_copies, piece_copies):
        for copy in copies:
            copy.wait_send()

    def sent(o):
        for copy in (edge_copy(o), sum_copy(o), weight_copy(o), whole_copy(o)):
            copy.wait_send()

    each(1, members, sent)
    each(1, chips, lambda d: back_copy(2 * d).wait_send())
    each(0, chips, lambda d: relay(d).wait_send())
    for copy in stores:
        copy.wait()


def hand_on(*refs):
    given, results, held, load_sem, store_sem = refs[:4], refs[4:8], refs[8:13], refs[13], refs[14]
    loads = [pltpu.make_async_copy(given[i], held[i], load_sem.at[i]) for i in range(4)]
    for load in loads:
        load.start()
    stores = []
    for i in (3, 0, 1, 2):
        loads[i].wait()
        source = held[i]
        if i == 2:
            source = held[4]
            source[...] = held[2][...].astype(F32).reshape(source.shape)
        stores.append(pltpu.make_async_copy(source, results[i], store_sem.at[i]))
        stores[-1].start()
    for copy in stores:
        copy.wait()


def per_device(
    reps, members, features, weight, bias, cotangent, degree, cols, edge_tile, edge_row, edge_col
):
    tile, width = features.shape
    depth = weight.shape[0]
    edges = edge_tile.shape[1]
    piece = depth // members
    args = (cols, features, weight, bias[None, :], cotangent, degree[None, :])
    args += (edge_tile, edge_row, edge_col)
    hbm = pl.BlockSpec(memory_space=pltpu.HBM)
    outs = (
        jax.ShapeDtypeStruct((tile, width), BF16),
        jax.ShapeDtypeStruct((tile, depth), BF16),
        jax.ShapeDtypeStruct((depth, width), F32),
        jax.ShapeDtypeStruct((1, width), F32),
    )
    given = outs[:2] + (jax.ShapeDtypeStruct((members, piece, width), BF16),) + outs[3:]
    results = pl.pallas_call(
        functools.partial(kernel, reps, members),
        out_shape=given,
        in_specs=[hbm] * len(args),
        out_specs=(hbm,) * 4,
        scratch_shapes=[pltpu.SMEM(cols.shape, cols.dtype)]
        + [pltpu.VMEM(a.shape, a.dtype) for a in args[1:] + outs[:2] + outs[3:]]
        + [
            pltpu.SemaphoreType.DMA((len(args),)),
            pltpu.SemaphoreType.DMA((4,)),
            pltpu.VMEM((3 * tile, 128), BF16),
            pltpu.VMEM((tile, edges), BF16),
            pltpu.VMEM((3 * tile, edges), BF16),
            pltpu.VMEM((members, 2, edges), jnp.int32),
            pltpu.VMEM((members, 3 * tile, tile), BF16),
            pltpu.VMEM((3 * tile, width), BF16),
            pltpu.VMEM((members, tile, width), BF16),
            pltpu.VMEM((members, tile, width), BF16),
            pltpu.VMEM((tile, width), F32),
            pltpu.VMEM((3 * tile, width), F32),
            pltpu.VMEM((members, tile + 16, width), BF16),
            pltpu.VMEM((2 * tile, width), BF16),
            pltpu.VMEM((2 * tile, width), BF16),
            pltpu.VMEM((members, piece, tile), BF16),
            pltpu.VMEM((members, piece, width), BF16),
            pltpu.VMEM((members, piece, width), BF16),
            pltpu.VMEM((piece, width), BF16),
            pltpu.VMEM((reps, piece, width), BF16),
            pltpu.VMEM((members, piece, width), BF16),
            pltpu.VMEM((8, width), F32),
            pltpu.VMEM((reps, 8, width), F32),
            pltpu.SemaphoreType.DMA((5, members)),
            pltpu.SemaphoreType.DMA((5, members)),
            pltpu.SemaphoreType.DMA((2, reps)),
            pltpu.SemaphoreType.DMA((2, reps)),
            pltpu.SemaphoreType.DMA((4,)),
            pltpu.SemaphoreType.DMA((4,)),
        ],
        compiler_params=pltpu.CompilerParams(
            collective_id=0, has_side_effects=True, vmem_limit_bytes=LIMIT
        ),
    )(*args)
    hidden, grad_features, grad_weight, grad_bias = pl.pallas_call(
        hand_on,
        out_shape=outs,
        in_specs=[hbm] * 4,
        out_specs=(hbm,) * 4,
        scratch_shapes=[pltpu.VMEM(a.shape, a.dtype) for a in given + outs[2:3]]
        + [pltpu.SemaphoreType.DMA((4,)), pltpu.SemaphoreType.DMA((4,))],
        compiler_params=pltpu.CompilerParams(vmem_limit_bytes=LIMIT),
    )(*results)
    return hidden, grad_features, grad_weight, grad_bias[0]


def solution(mesh):
    nodes = P(("rep", "grp"), None)
    return jax.shard_map(
        functools.partial(per_device, mesh.shape["rep"], mesh.shape["grp"]),
        mesh=mesh,
        in_specs=(nodes, P(), P(), nodes, P(("rep", "grp")), nodes, nodes, nodes, nodes),
        out_specs=(nodes, nodes, P(), P()),
        check_vma=False,
    )
```

```python
import functools

import jax
import jax.numpy as jnp
from jax import lax
from jax.experimental import pallas as pl
from jax.experimental.pallas import tpu as pltpu
from jax.sharding import PartitionSpec as P

MESH = pl.DeviceIdType.MESH
F32 = jnp.float32
BF16 = jnp.bfloat16
F8 = jnp.float8_e4m3fn
LIMIT = 63 * 2**20
ROWS = (((0,), (0,)), ((), ()))
LANES = (((1,), (1,)), ((), ()))


def mm(a, b, dims=(((1,), (0,)), ((), ()))):
    return lax.dot_general(a, b, dims, preferred_element_type=F32)


def kernel(
    reps,
    members,
    cols_hbm,
    features_hbm,
    weight_hbm,
    bias_hbm,
    cotangent_hbm,
    degree_hbm,
    edge_tile_hbm,
    edge_row_hbm,
    edge_col_hbm,
    hidden_hbm,
    grad_features_hbm,
    grad_weight_hbm,
    grad_bias_hbm,
    cols_ref,
    features_ref,
    weight_ref,
    bias_ref,
    cotangent_ref,
    degree_ref,
    edge_tile_ref,
    edge_row_ref,
    edge_col_ref,
    hidden_ref,
    grad_features_ref,
    grad_bias_ref,
    load_sem,
    store_sem,
    spots,
    left_hot,
    right_hot,
    listed,
    tiles_t,
    scaled,
    sums_out,
    sums,
    own_sum,
    grads,
    back,
    parts_out,
    parts,
    features_t,
    weight_out,
    weight_in,
    piece_out,
    piece_in,
    whole,
    bias_sum,
    bias_near,
    grp_send,
    grp_recv,
    rep_send,
    rep_recv,
    near_send,
    near_recv,
):
    rep = lax.axis_index("rep")
    me = lax.axis_index("grp")
    tile, width = features_ref.shape
    half = tile // 2
    edges = edge_tile_ref.shape[1]
    piece = whole.shape[1]
    chips = members // 2
    chip, core = me // 2, me % 2

    def mate(o):
        d, s = o // 2, o % 2
        return (chip + d) % chips * 2 + (core + s) % 2

    def source(o):
        d, s = o // 2, o % 2
        return (chip + chips - d) % chips * 2 + (core + s) % 2

    def reply(o):
        return (chips - o // 2) % chips * 2 + o % 2

    def peer(o):
        return (rep + o) % reps

    barrier = pltpu.get_barrier_semaphore()
    for o in range(1, members):
        pl.semaphore_signal(barrier, inc=1, device_id={"grp": mate(o)}, device_id_type=MESH)
    for o in range(1, reps):
        pl.semaphore_signal(barrier, inc=1, device_id={"rep": peer(o)}, device_id_type=MESH)
    pairs = (
        (cols_hbm, cols_ref),
        (edge_tile_hbm, edge_tile_ref),
        (edge_row_hbm, edge_row_ref),
        (edge_col_hbm, edge_col_ref),
        (features_hbm, features_ref),
        (weight_hbm, weight_ref),
        (degree_hbm, degree_ref),
        (bias_hbm, bias_ref),
        (cotangent_hbm, cotangent_ref),
    )
    loads = [
        pltpu.make_async_copy(a, b, load_sem.at[i]) for i, (a, b) in enumerate(pairs)
    ]
    for load in loads:
        load.start()

    def remote(src, dst, send, recv, to):
        return pltpu.make_async_remote_copy(
            src_ref=src,
            dst_ref=dst,
            send_sem=send,
            recv_sem=recv,
            device_id=to,
            device_id_type=MESH,
        )

    def to_mate(stage, o, src, dst):
        send, recv = grp_send.at[stage, o], grp_recv.at[stage, o]
        return remote(src, dst, send, recv, {"grp": mate(o)})

    def to_near(slot, o, src, dst):
        return remote(src, dst, near_send.at[slot], near_recv.at[slot], {"rep": peer(o)})

    def store(i, src, dst):
        copy = pltpu.make_async_copy(src, dst, store_sem.at[i])
        copy.start()
        return copy

    def each(first, last, act):
        def body(i, _):
            act(i)
            return 0

        lax.fori_loop(first, last, body, 0)

    def begin(copies):
        for copy in copies:
            copy.start()
        return copies

    for load in loads[:4]:
        load.wait()
    edge_tile = edge_tile_ref[...]
    column = jnp.zeros_like(edge_tile)
    for t in range(cols_ref.shape[1]):
        column = jnp.where(edge_tile == t, cols_ref[0, t], column)
    listed[0, pl.ds(0, 1), :] = edge_row_ref[...]
    listed[0, pl.ds(1, 1), :] = column * tile + edge_col_ref[...]
    pl.semaphore_wait(barrier, members + reps - 2)

    def edge_copy(o):
        return to_mate(0, o, listed.at[0], listed.at[o])

    each(1, members, lambda o: edge_copy(o).start())

    for load in loads[4:]:
        load.wait()
    dinv = lax.rsqrt(degree_ref[...].astype(F32))
    dinv = jnp.broadcast_to(dinv, (tile, tile)).T
    dinv = jnp.concatenate([dinv] * (width // tile), axis=1)

    own = pl.ds(tile, tile)
    scaled[own, :] = (mm(features_ref[...], weight_ref[...]) * dinv).astype(BF16)
    scaled_copies = begin(
        [
            to_near(0, 1, scaled.at[own], scaled.at[pl.ds(0, tile)]),
            to_near(1, reps - 1, scaled.at[own], scaled.at[pl.ds(2 * tile, tile)]),
        ]
    )
    features_t[...] = (
        features_ref[...].astype(F32).T.reshape(features_t.shape).astype(BF16)
    )
    spots[...] = lax.broadcasted_iota(jnp.int32, spots.shape, 0).astype(F32).astype(BF16)

    span = edges // 5 if edges % 640 == 0 else edges

    def count(o):
        row = listed[o, pl.ds(0, 1), :]
        window = listed[o, pl.ds(1, 1), :]
        column = window // tile
        part = (column >= members).astype(jnp.int32) + (column >= 2 * members).astype(jnp.int32)
        place = window - column * tile
        upper = (place >= half).astype(jnp.int32)
        left = jnp.where(column - part * members == me, upper * tile + row, -1)
        right = part * half + place - upper * half
        total = None
        for first in range(0, edges, span):
            at = pl.ds(first, span)
            for hot, key in ((left_hot, left), (right_hot, right)):
                rows = hot.shape[0]
                key = key[:, first : first + span].astype(F32)
                key = jnp.broadcast_to(key, (16, span)).astype(BF16)
                key = jnp.concatenate([key] * (rows // 16), axis=0)
                spot = jnp.concatenate([spots[:rows]] * (span // 128), axis=1)
                hit = jnp.where(spot == key, jnp.ones_like(key), jnp.zeros_like(key))
                hot[:, at] = hit.astype(hot.dtype)
            term = mm(right_hot[:, at], left_hot[:, at], LANES)
            total = term if total is None else total + term
        total = total.astype(BF16)
        blocks = [
            total[p * half : (p + 1) * half, u * tile : (u + 1) * tile]
            for p in range(3)
            for u in range(2)
        ]
        return jnp.concatenate(blocks, axis=0)

    def sum_copy(o):
        return to_mate(1, reply(o), sums_out.at[o], sums.at[reply(o)])

    def forward(o):
        @pl.when(o > 0)
        def _():
            edge_copy(o).wait_recv()

        tiles_t[o] = count(o)

        @pl.when(o == 0)
        def _():
            for copy in scaled_copies:
                copy.wait_recv()

        term = mm(tiles_t[o], scaled[...], ROWS)

        @pl.when(o == 0)
        def _():
            own_sum[...] = term

        @pl.when(o > 0)
        def _():
            sums_out[o] = term.astype(BF16)
            sum_copy(o).start()

    each(0, members, forward)

    def add_sum(o, total):
        to_mate(1, o, sums_out.at[o], sums.at[o]).wait_recv()
        return total + sums[o].astype(F32)

    total = lax.fori_loop(1, members, add_sum, own_sum[...])
    pre = total * dinv + bias_ref[...]
    sig = jax.nn.sigmoid(pre)
    grad_pre = cotangent_ref[...].astype(F32) * sig * (1.0 + pre * (1.0 - sig))
    back[0, pl.ds(0, tile), :] = (grad_pre * dinv).astype(BF16)
    bias_part = jnp.broadcast_to(jnp.sum(grad_pre, axis=0, keepdims=True), (8, width))
    bias_high = bias_part.astype(BF16).astype(F32)
    bias_rows = jnp.concatenate([bias_high, bias_part - bias_high], axis=0)
    back[0, pl.ds(tile, 16), :] = bias_rows.astype(BF16)
    def back_copy(o):
        return to_mate(2, o, back.at[0], back.at[o])

    def relay(d):
        send, recv = grp_send.at[2, 2 * d + 1], grp_recv.at[2, 2 * d + 1]
        return remote(back.at[2 * d], back.at[2 * d + 1], send, recv, {"grp": mate(1)})

    each(1, chips, lambda d: back_copy(2 * d).start())
    back_copy(1).start()
    hidden_ref[...] = (pre * sig).astype(BF16)
    stores = [store(0, hidden_ref, hidden_hbm)]

    def grad_term(o):
        return mm(tiles_t[o], back[o, pl.ds(0, tile), :])

    grads[...] = grad_term(0)

    def grad_across(d):
        back_copy(2 * d).wait_recv()
        relay(d).start()
        grads[...] += grad_term(2 * d)

    def grad_beside(d):
        relay(d).wait_recv()
        grads[...] += grad_term(2 * d + 1)

    each(1, chips, grad_across)
    each(0, chips, grad_beside)
    parts_out[pl.ds(0, tile), :] = grads[:tile, :].astype(BF16)
    parts_out[pl.ds(tile, tile), :] = grads[2 * tile :, :].astype(BF16)
    lower, upper = pl.ds(0, tile), pl.ds(tile, tile)
    part_copies = begin(
        [
            to_near(2, reps - 1, parts_out.at[lower], parts.at[lower]),
            to_near(3, 1, parts_out.at[upper], parts.at[upper]),
        ]
    )
    bias_rows = jnp.zeros((16, width), F32)
    for o in range(members):
        bias_rows = bias_rows + back[o, pl.ds(tile, 16), :].astype(F32)
    bias_total = bias_rows[:8] + bias_rows[8:]
    bias_sum[...] = bias_total
    bias_copies = begin(
        [
            remote(bias_sum, bias_near.at[o], rep_send.at[1, o], rep_recv.at[1, o], {"rep": peer(o)})
            for o in range(1, reps)
        ]
    )
    for copy in part_copies:
        copy.wait_recv()
    grad_sum = grads[tile : 2 * tile, :] + parts[lower, :].astype(F32) + parts[upper, :].astype(F32)
    grad_scaled = (grad_sum * dinv).astype(BF16)

    def weight_copy(o):
        return to_mate(3, o, weight_out.at[o], weight_in.at[o])

    def weight_piece(o):
        weight_out[o] = mm(features_t[mate(o)], grad_scaled).astype(BF16)
        weight_copy(o).start()

    each(1, members, weight_piece)
    total = mm(features_t[me], grad_scaled)
    grad_features_ref[...] = mm(grad_scaled, weight_ref[...], LANES).astype(BF16)
    stores.append(store(1, grad_features_ref, grad_features_hbm))
    for o, copy in enumerate(bias_copies, 1):
        copy.wait_recv()
        bias_total = bias_total + bias_near[o]
    grad_bias_ref[...] = bias_total[:1]
    stores.append(store(2, grad_bias_ref, grad_bias_hbm))

    def add_piece(o, total):
        weight_copy(o).wait_recv()
        return total + weight_in[o].astype(F32)

    total = lax.fori_loop(1, members, add_piece, total)
    piece_out[...] = total.astype(BF16)
    piece_copies = begin(
        [
            remote(
                piece_out, piece_in.at[o], rep_send.at[0, o], rep_recv.at[0, o], {"rep": peer(o)}
            )
            for o in range(1, reps)
        ]
    )
    for o, copy in enumerate(piece_copies, 1):
        copy.wait_recv()
    piece_in[0] = piece_out[...]
    total = piece_in[rep].astype(F32)
    for k in range(1, reps):
        total = total + piece_in[(rep - k + reps) % reps].astype(F32)
    whole[me] = total.astype(whole.dtype)

    def whole_copy(o):
        return to_mate(4, o, whole.at[me], whole.at[me])

    each(1, members, lambda o: whole_copy(o).start())
    each(1, members, lambda o: whole_copy(o).wait_recv())
    stores.append(store(3, whole, grad_weight_hbm))

    for copies in (scaled_copies, bias_copies, part_copies, piece_copies):
        for copy in copies:
            copy.wait_send()

    def sent(o):
        for copy in (edge_copy(o), sum_copy(o), weight_copy(o), whole_copy(o)):
            copy.wait_send()

    each(1, members, sent)
    each(1, chips, lambda d: back_copy(2 * d).wait_send())
    each(0, chips, lambda d: relay(d).wait_send())
    for copy in stores:
        copy.wait()


def hand_on(*refs):
    given, results, held, load_sem, store_sem = refs[:4], refs[4:8], refs[8:13], refs[13], refs[14]
    loads = [pltpu.make_async_copy(given[i], held[i], load_sem.at[i]) for i in range(4)]
    for load in loads:
        load.start()
    stores = []
    for i in (3, 0, 1, 2):
        loads[i].wait()
        source = held[i]
        if i == 2:
            source = held[4]
            source[...] = held[2][...].astype(F32).reshape(source.shape)
        stores.append(pltpu.make_async_copy(source, results[i], store_sem.at[i]))
        stores[-1].start()
    for copy in stores:
        copy.wait()


def per_device(
    reps, members, features, weight, bias, cotangent, degree, cols, edge_tile, edge_row, edge_col
):
    tile, width = features.shape
    depth = weight.shape[0]
    edges = edge_tile.shape[1]
    piece = depth // members
    args = (cols, features, weight, bias[None, :], cotangent, degree[None, :])
    args += (edge_tile, edge_row, edge_col)
    hbm = pl.BlockSpec(memory_space=pltpu.HBM)
    outs = (
        jax.ShapeDtypeStruct((tile, width), BF16),
        jax.ShapeDtypeStruct((tile, depth), BF16),
        jax.ShapeDtypeStruct((depth, width), F32),
        jax.ShapeDtypeStruct((1, width), F32),
    )
    given = outs[:2] + (jax.ShapeDtypeStruct((members, piece, width), BF16),) + outs[3:]
    results = pl.pallas_call(
        functools.partial(kernel, reps, members),
        out_shape=given,
        in_specs=[hbm] * len(args),
        out_specs=(hbm,) * 4,
        scratch_shapes=[pltpu.SMEM(cols.shape, cols.dtype)]
        + [pltpu.VMEM(a.shape, a.dtype) for a in args[1:] + outs[:2] + outs[3:]]
        + [
            pltpu.SemaphoreType.DMA((len(args),)),
            pltpu.SemaphoreType.DMA((4,)),
            pltpu.VMEM((2 * tile, 128), BF16),
            pltpu.VMEM((2 * tile, edges), F8),
            pltpu.VMEM((3 * tile // 2, edges), F8),
            pltpu.VMEM((members, 2, edges), jnp.int32),
            pltpu.VMEM((members, 3 * tile, tile), BF16),
            pltpu.VMEM((3 * tile, width), BF16),
            pltpu.VMEM((members, tile, width), BF16),
            pltpu.VMEM((members, tile, width), BF16),
            pltpu.VMEM((tile, width), F32),
            pltpu.VMEM((3 * tile, width), F32),
            pltpu.VMEM((members, tile + 16, width), BF16),
            pltpu.VMEM((2 * tile, width), BF16),
            pltpu.VMEM((2 * tile, width), BF16),
            pltpu.VMEM((members, piece, tile), BF16),
            pltpu.VMEM((members, piece, width), BF16),
            pltpu.VMEM((members, piece, width), BF16),
            pltpu.VMEM((piece, width), BF16),
            pltpu.VMEM((reps, piece, width), BF16),
            pltpu.VMEM((members, piece, width), BF16),
            pltpu.VMEM((8, width), F32),
            pltpu.VMEM((reps, 8, width), F32),
            pltpu.SemaphoreType.DMA((5, members)),
            pltpu.SemaphoreType.DMA((5, members)),
            pltpu.SemaphoreType.DMA((2, reps)),
            pltpu.SemaphoreType.DMA((2, reps)),
            pltpu.SemaphoreType.DMA((4,)),
            pltpu.SemaphoreType.DMA((4,)),
        ],
        compiler_params=pltpu.CompilerParams(
            collective_id=0, has_side_effects=True, vmem_limit_bytes=LIMIT
        ),
    )(*args)
    hidden, grad_features, grad_weight, grad_bias = pl.pallas_call(
        hand_on,
        out_shape=outs,
        in_specs=[hbm] * 4,
        out_specs=(hbm,) * 4,
        scratch_shapes=[pltpu.VMEM(a.shape, a.dtype) for a in given + outs[2:3]]
        + [pltpu.SemaphoreType.DMA((4,)), pltpu.SemaphoreType.DMA((4,))],
        compiler_params=pltpu.CompilerParams(vmem_limit_bytes=LIMIT),
    )(*results)
    return hidden, grad_features, grad_weight, grad_bias[0]


def solution(mesh):
    nodes = P(("rep", "grp"), None)
    return jax.shard_map(
        functools.partial(per_device, mesh.shape["rep"], mesh.shape["grp"]),
        mesh=mesh,
        in_specs=(nodes, P(), P(), nodes, P(("rep", "grp")), nodes, nodes, nodes, nodes),
        out_specs=(nodes, nodes, P(), P()),
        check_vma=False,
    )
```
